512 devices in a mesh: dp: 16 (over x_lo, y, core), expert: 32 (over z, x_hi).
Axes of the slice: x: 4 (x_hi: 2, x_lo: 2; x = x_hi * 2 + x_lo), y: 4, z: 16, core: 2. Of those that a mesh axis runs over, the one named last changes fastest.
Arguments:
- grad_out: bfloat16 [16384, 2048], P(('dp', 'expert')), may hold values from -6 to 6
- expert_ids: int32 [16384, 8], P(('dp', 'expert')), may hold values from 0 to 31, all different within a row; in each aligned block of 32 rows (0 to 31, 32 to 63, ...) at most 12 rows name the same one
- route_weights: bfloat16 [16384, 8], P(('dp', 'expert')), may hold values from 0.049804688 to 0.5
- saved_pre: bfloat16 [16, 32, 384, 1536], P('dp', 'expert'), may hold values from -6 to 6
- gate_weight: bfloat16 [32, 2048, 768], P('expert', 'dp'), may hold values from -0.125 to 0.125
- up_weight: bfloat16 [32, 2048, 768], P('expert', 'dp'), may hold values from -0.125 to 0.125
- down_weight: bfloat16 [32, 768, 2048], P('expert', 'dp'), may hold values from -0.21875 to 0.21875
Outputs:
- token_grad: bfloat16 [16384, 2048], P(('dp', 'expert'))
- route_grad: bfloat16 [16384, 8], P(('dp', 'expert'))
- down_grad: bfloat16 [32, 768, 2048], P('expert', 'dp')
The draws below stay inside these ranges and needn't reach their ends.
Inputs may be any that keep to these rules, and one draw needn't show every extreme that they name: `expert_ids`: each row names 8 different experts. Among the 32 rows of one device no expert is named by more than 12 rows, a bound that some block reaches.
All inputs are finite; a program needn't handle non-finite values.
Results may differ from the reference program's by a relative error of at most 0.023.
Values may be sent and summed in bfloat16 or wider, within the bound.
No kernel may reach another device: no remote copies, remote signals or barrier semaphores. Data moves between devices by JAX's collectives and lax.ppermute only.
A program may use at most 64 MiB of HBM per device.

```python
import math
import jax
import jax.numpy as jnp
import numpy as np
from jax import lax

D = 2048
H = 768
TOPK = 8
TOK_DEV = 32
EXPERTS = 32
CAP = 12
SLOTS = 384
GROUPS = 16
TOKENS = 16384
N_DP = 16
N_EXPERT = 32


def levels(stream_key, shape, split, low, largest):
    def one(axis_at, parts):
        heights = jax.random.uniform(jax.random.fold_in(jax.random.fold_in(stream_key, 6), axis_at), (parts,), jnp.float32, low / len(split), largest / len(split))
        return jnp.repeat(jnp.exp(heights), shape[axis_at] // parts).reshape((-1,) + (1,) * (len(shape) - axis_at - 1))

    gain = one(*split[0])
    for cut in split[1:]:
        gain = gain * one(*cut)
    return gain


def assign_block(stream_key, own, number, rows, amount, top, reach, skew):
    order = jax.random.permutation(stream_key, amount)
    heavy_load, usual = shares(amount, rows * top, reach, skew, True), shares(amount, rows * top, reach, skew, False)
    places = jnp.arange(amount)

    def named(sizes, turn):
        used = int((sizes > 0).sum())
        fixed = max(1, used // 4)
        shifted = fixed + (places - fixed + turn * (used - fixed)) % max(1, amount - fixed)
        return jnp.zeros((amount,), jnp.int32).at[order[jnp.where(places < fixed, places, shifted)]].set(jnp.asarray(sizes, jnp.int32))

    sizes = jnp.where(number % 4 == 0, named(heavy_load, number // 4), named(usual, number - number // 4 - 1))
    mixed = jax.random.permutation(jax.random.fold_in(own, 3), amount)
    source_of, sink = mixed[0:amount // 2 * 2:2], mixed[1:amount // 2 * 2:2]
    slack = jnp.minimum(sizes[source_of] - 1, reach - sizes[sink]) // 2
    slack = jnp.where((source_of == order[0]) | (sink == order[0]) | (sizes[sink] == 0), 0, jnp.maximum(slack, 0))
    shifted = jax.random.randint(jax.random.fold_in(own, 4), (amount // 2,), 0, 1 << 20) % (slack + 1)
    sizes = sizes.at[source_of].add(-shifted).at[sink].add(shifted)
    items = jnp.searchsorted(jnp.cumsum(sizes), jnp.arange(rows * top), side="right").astype(jnp.int32)
    grid = items.reshape(top, rows).T
    grid = grid[jax.random.permutation(jax.random.fold_in(own, 1), rows)]
    turn = jax.random.randint(jax.random.fold_in(own, 2), (rows, 1), 0, top)
    return jnp.take_along_axis(grid, (jnp.arange(top)[None, :] + turn) % top, axis=1)


def shares(number_of, total, reach, slope, full):
    portions = [(1 << 20) // math.isqrt(standing ** slope) + 1 for standing in range(1, number_of + 1)]
    largest = reach if full else min(reach, max(-(-total // number_of), total * portions[0] // sum(portions)))
    least = 1 if total - largest >= number_of - 1 else 0
    holding, surplus = [largest] + [least] * (number_of - 1), total - largest - least * (number_of - 1)
    while surplus > 0:
        free = [i for i in range(1, number_of) if holding[i] < largest] or [i for i in range(1, number_of) if holding[i] < reach]
        mass, left = sum([portions[i] for i in free]), surplus
        for i in free:
            more = min(reach - holding[i], max(1, left * portions[i] // mass), surplus)
            holding[i] = holding[i] + more
            surplus = surplus - more
    return np.array(holding)


def scatter_about(rng, shape, deviation, reach, cuts=(), kind=jnp.bfloat16):
    entries = deviation * jax.random.normal(rng, shape, jnp.float32)
    if cuts:
        entries = entries * levels(rng, shape, cuts, -0.22, 0.18)
    return jnp.clip(entries, -reach, reach).astype(kind)


def setup_inputs(seed: int = 0) -> dict:
    keys = jax.random.split(jax.random.key(seed), 8)
    grad_out = scatter_about(keys[0], (TOKENS, D), 1.0, 6.0, ((0, 512),))
    expert_ids_keys = jax.random.split(jax.random.fold_in(keys[1], 1), TOKENS // TOK_DEV)
    expert_ids_turns = jax.random.permutation(jax.random.fold_in(keys[1], 3), TOKENS // TOK_DEV)
    expert_ids = jax.vmap(lambda own, number: assign_block(jax.random.fold_in(keys[1], 2), own, number, TOK_DEV, EXPERTS, TOPK, CAP, 2))(expert_ids_keys, expert_ids_turns).reshape((TOKENS, TOPK))
    route_weights = jnp.clip(jnp.exp(math.log(0.5) - 2.306499 * jax.random.uniform(keys[2], (TOKENS, TOPK), jnp.float32) ** levels(keys[2], (TOKENS, TOPK), ((0, 512),), -0.2, 0.2)), 0.049804688, 0.5).astype(jnp.bfloat16)
    saved_pre = scatter_about(keys[3], (GROUPS, EXPERTS, SLOTS, 2 * H), 1.0, 6.0, ((0, 16), (1, 32)))
    gate_weight = scatter_about(keys[4], (EXPERTS, D, H), D ** -0.5, 0.125, ((0, 32), (1, 16)))
    up_weight = scatter_about(keys[5], (EXPERTS, D, H), D ** -0.5, 0.125, ((0, 32), (1, 16)))
    down_weight = scatter_about(keys[6], (EXPERTS, H, D), H ** -0.5, 0.21875, ((0, 32), (1, 16)))
    return {"grad_out": grad_out, "expert_ids": expert_ids, "route_weights": route_weights, "saved_pre": saved_pre, "gate_weight": gate_weight, "up_weight": up_weight, "down_weight": down_weight}


def reference(grad_out, expert_ids, route_weights, saved_pre, gate_weight, up_weight, down_weight):
    blocks = N_DP * N_EXPERT
    ids_block = expert_ids.reshape(blocks, TOK_DEV, TOPK)
    matches = (ids_block[..., None] == jnp.arange(EXPERTS, dtype=jnp.int32)).astype(jnp.int32)
    members = jnp.sum(matches, axis=2)
    rank_tok = jnp.cumsum(members, axis=1) - members
    rank_used = jnp.where(members > 0, rank_tok, CAP).astype(jnp.int32)
    shape_full = (blocks, TOK_DEV, EXPERTS)
    block_idx = jnp.broadcast_to(jnp.arange(blocks, dtype=jnp.int32)[:, None, None], shape_full)
    expert_idx = jnp.broadcast_to(jnp.arange(EXPERTS, dtype=jnp.int32)[None, None, :], shape_full)
    token_idx = jnp.broadcast_to(jnp.arange(TOKENS, dtype=jnp.int32).reshape(blocks, TOK_DEV)[:, :, None], shape_full)
    table = jnp.full((blocks, EXPERTS, CAP), TOKENS, jnp.int32)
    table = table.at[block_idx, expert_idx, rank_used].set(token_idx, mode="drop")
    weight_te = jnp.sum(route_weights.astype(jnp.float32).reshape(blocks, TOK_DEV, TOPK)[..., None] * matches, axis=2)
    weight_table = jnp.zeros((blocks, EXPERTS, CAP), jnp.float32)
    weight_table = weight_table.at[block_idx, expert_idx, rank_used].set(weight_te, mode="drop")
    slot_rows = jnp.transpose(table.reshape(N_DP, N_EXPERT, EXPERTS, CAP), (2, 0, 1, 3)).reshape(EXPERTS, N_DP, SLOTS)
    slot_weights = jnp.transpose(weight_table.reshape(N_DP, N_EXPERT, EXPERTS, CAP), (2, 0, 1, 3)).reshape(EXPERTS, N_DP, SLOTS)
    padded = jnp.concatenate([grad_out, jnp.zeros((1, D), jnp.bfloat16)], axis=0)
    pre_by_expert = jnp.moveaxis(saved_pre, 1, 0)

    def one_expert(carry, inputs):
        dx_acc, route_acc = carry
        expert, rows_e, weight_e, pre_e, gate_e, up_e, down_e = inputs
        slot_y = padded[rows_e]
        gate_pre = pre_e[..., :H].astype(jnp.float32)
        up_pre = pre_e[..., H:].astype(jnp.float32)
        sigmoid_gate = jax.nn.sigmoid(gate_pre)
        silu_gate = gate_pre * sigmoid_gate
        hidden_act = (silu_gate * up_pre).astype(jnp.bfloat16)
        hidden_f32 = lax.optimization_barrier(hidden_act).astype(jnp.float32)
        q_slot = jnp.einsum("gsd,hd->gsh", slot_y.astype(jnp.float32), down_e.astype(jnp.float32))
        scaled = (weight_e[..., None] * slot_y.astype(jnp.float32)).astype(jnp.bfloat16)
        partials = jnp.einsum("gsh,gsd->ghd", hidden_f32, scaled.astype(jnp.float32)).astype(jnp.bfloat16)
        down_e_grad = jnp.sum(partials.astype(jnp.float32), axis=0).astype(jnp.bfloat16)
        slot_route = jnp.sum(q_slot * hidden_f32, axis=-1).astype(jnp.bfloat16)
        grad_hidden = weight_e[..., None] * q_slot
        grad_gate = grad_hidden * up_pre * sigmoid_gate * (1.0 + gate_pre * (1.0 - sigmoid_gate))
        grad_up = grad_hidden * silu_gate
        grad_both = jnp.concatenate([grad_gate, grad_up], axis=-1).astype(jnp.bfloat16)
        gate_up = jnp.concatenate([gate_e, up_e], axis=1)
        slot_dx = jnp.einsum("gsk,dk->gsd", grad_both.astype(jnp.float32), gate_up.astype(jnp.float32)).astype(jnp.bfloat16)
        flat_rows = rows_e.reshape(-1)
        dx_acc = dx_acc.at[flat_rows].add(slot_dx.reshape(-1, D).astype(jnp.float32))
        column = jnp.full_like(flat_rows, expert)
        route_acc = route_acc.at[flat_rows, column].set(slot_route.reshape(-1).astype(jnp.float32))
        return (dx_acc, route_acc), down_e_grad

    start = (jnp.zeros((TOKENS + 1, D), jnp.float32), jnp.zeros((TOKENS + 1, EXPERTS), jnp.float32))
    inputs = (jnp.arange(EXPERTS, dtype=jnp.int32), slot_rows, slot_weights, pre_by_expert, gate_weight, up_weight, down_weight)
    (dx_acc, route_acc), down_grad = lax.scan(one_expert, start, inputs)
    token_grad = dx_acc[:TOKENS].astype(jnp.bfloat16)
    route_grad = jnp.take_along_axis(route_acc[:TOKENS], expert_ids, axis=1).astype(jnp.bfloat16)
    return token_grad, route_grad, down_grad
```

```python
import functools

import jax
import jax.numpy as jnp
from jax import lax
from jax.experimental import pallas as pl
from jax.experimental.pallas import tpu as pltpu
from jax.sharding import PartitionSpec as P

BF16, F32 = jnp.bfloat16, jnp.float32
META = 128
STRIDE = 4
VMEM = 48 * 1024 * 1024


def params():
    return pltpu.CompilerParams(vmem_limit_bytes=VMEM)


def prep_kernel(rows_ref, ids_ref, weight_ref, gate_ref, up_ref, down_ref, tok_ref, pack_ref):
    tok, width = rows_ref.shape
    topk = ids_ref.shape[1]
    packed = down_ref.shape[0]
    hidden = gate_ref.shape[1]
    part = 2 * hidden * META // width
    tok_ref[:, :width] = rows_ref[...]
    meta = jnp.concatenate(
        [ids_ref[...].astype(F32), weight_ref[...].astype(F32), jnp.zeros((tok, META - 2 * topk), F32)], axis=1
    )
    tok_ref[:, width:] = meta.astype(BF16)
    for at, ref in enumerate((gate_ref, up_ref)):
        turned = ref[...].astype(F32).T.astype(BF16)
        for g in range(hidden // part):
            lane = (at * (hidden // part) + g) * META
            pack_ref[0:part, lane : lane + META] = turned[g * part : (g + 1) * part]
    pack_ref[part : part + packed, :] = down_ref[...]


def select_kernel(cap, mine_ref, tok_ref, send_ref, select_ref):
    rows, full = tok_ref.shape
    width = full - META
    dests, per, _ = send_ref.shape
    block = rows // STRIDE
    topk = 8
    ids = tok_ref[:, width:].astype(F32).T[0:topk, :]
    member = jnp.concatenate(
        [
            jnp.max((ids == mine_ref[j].astype(F32)).astype(F32), axis=0, keepdims=True)
            for j in range(dests)
        ],
        axis=0,
    )
    before = lax.broadcasted_iota(jnp.int32, (rows, rows), 0)
    after = lax.broadcasted_iota(jnp.int32, (rows, rows), 1)
    earlier = (before < after) & (before // block == after // block)
    rank = jnp.dot(member.astype(BF16), earlier.astype(BF16), preferred_element_type=F32)
    key = jnp.where(member > 0.0, rank, -1.0)
    place = lax.broadcasted_iota(jnp.int32, (per, rows), 0)
    source = lax.broadcasted_iota(jnp.int32, (per, rows), 1) // block
    pattern = jnp.where(place // cap == source, place - source * cap, -2).astype(F32)
    for j in range(dests):
        chosen = (key[j : j + 1, :] == pattern).astype(BF16)
        select_ref[j * per : (j + 1) * per, :] = chosen
    for j in range(dests):
        send_ref[j] = jnp.dot(
            select_ref[j * per : (j + 1) * per, :], tok_ref[...], preferred_element_type=F32
        ).astype(BF16)


def act_kernel(cap, pre_ref, hid_ref, turned_ref, slope_ref, silu_ref):
    slots, both = pre_ref.shape
    hidden = both // 2
    dests = slots // (cap * STRIDE)
    at = lax.broadcasted_iota(jnp.int32, (slots, slots), 0)
    src = lax.broadcasted_iota(jnp.int32, (slots, slots), 1)
    j, rest = at // (STRIDE * cap), at % (STRIDE * cap)
    k, r = rest // cap, rest % cap
    order = (src == (k * dests + j) * cap + r).astype(BF16)
    a = jnp.dot(order, pre_ref[:, :hidden], preferred_element_type=F32)
    u = jnp.dot(order, pre_ref[:, hidden:], preferred_element_type=F32)
    sig = jax.nn.sigmoid(a)
    silu = a * sig
    hid = (silu * u).astype(BF16)
    hid_ref[...] = hid
    turned_ref[...] = hid.astype(F32).T.astype(BF16)
    slope_ref[...] = u * sig * (1.0 + a * (1.0 - sig))
    silu_ref[...] = silu


def slot_weight(meta, expert):
    topk = 8
    meta = meta.astype(F32)
    lane = lax.broadcasted_iota(jnp.int32, meta.shape, 1)
    weight = pltpu.roll(meta, META - topk, 1)
    return jnp.sum(jnp.where((lane < topk) & (meta == expert.astype(F32)), weight, 0.0), axis=1, keepdims=True)


def down_kernel(mine_ref, got_ref, meta_ref, turned_ref, out_ref):
    w = slot_weight(meta_ref[...], mine_ref[0])
    scaled = (w * got_ref[...].astype(F32)).astype(BF16)
    out_ref[...] = jnp.dot(turned_ref[...], scaled, preferred_element_type=F32).astype(BF16)


def mid_kernel(mine_ref, got_ref, hid_ref, slope_ref, silu_ref, down_ref, pack_ref, out_ref, both_ref, wide_ref):
    step = pl.program_id(0)
    width = got_ref.shape[1] - META
    hidden = hid_ref.shape[1]
    pair, part, _ = pack_ref.shape

    @pl.when(step == 0)
    def _():
        w = slot_weight(got_ref[:, width:], mine_ref[0])
        q = lax.dot_general(
            got_ref[:, :width],
            down_ref[...].reshape(hidden, width),
            (((1,), (1,)), ((), ())),
            preferred_element_type=F32,
        )
        route = jnp.sum(q * hid_ref[...].astype(F32), axis=1, keepdims=True)
        grad = w * q
        both_ref[:, :hidden] = (grad * slope_ref[...]).astype(BF16)
        both_ref[:, hidden:] = (grad * silu_ref[...]).astype(BF16)
        lane = lax.broadcasted_iota(jnp.int32, (got_ref.shape[0], META), 1)
        out_ref[:, width:] = jnp.where(lane == mine_ref[0], route, 0.0).astype(BF16)

    @pl.when(step > 0)
    def _():
        for b in range(pair):
            for g in range(2 * hidden // part):
                wide_ref[g * part : (g + 1) * part, b * META : (b + 1) * META] = pack_ref[
                    b, :, g * META : (g + 1) * META
                ]
        at = pl.multiple_of((step - 1) * (pair * META), pair * META)
        out_ref[:, pl.ds(at, pair * META)] = jnp.dot(
            both_ref[...], wide_ref[...], preferred_element_type=F32
        ).astype(BF16)


def combine_kernel(select_ref, back_ref, out_ref):
    total = lax.dot_general(
        select_ref[...], back_ref[...], (((0,), (0,)), ((), ())), preferred_element_type=F32
    )
    out_ref[...] = total.astype(BF16)


def last_kernel(part_ref, ids_ref, tok_ref, route_ref):
    width = tok_ref.shape[1]
    total = part_ref[0].astype(F32)
    for k in range(1, STRIDE):
        total = total + part_ref[k].astype(F32)
    tok_ref[...] = total[:, :width].astype(BF16)
    route = total[:, width:]
    ids = ids_ref[...]
    lane = lax.broadcasted_iota(jnp.int32, route.shape, 1)
    found = [
        jnp.sum(jnp.where(lane == ids[:, k : k + 1], route, 0.0), axis=1, keepdims=True)
        for k in range(ids.shape[1])
    ]
    route_ref[...] = jnp.concatenate(found, axis=1).astype(BF16)


def shape(dims, dtype=BF16):
    return jax.ShapeDtypeStruct(dims, dtype)


def whole(memory=pltpu.VMEM):
    return pl.BlockSpec(memory_space=memory)


def per_device(n_dp, n_expert, grad_out, expert_ids, route_weights, saved_pre, gate_weight, up_weight, down_weight):
    tok, width = grad_out.shape
    pre = saved_pre[0, 0]
    slots, both = pre.shape
    hidden = both // 2
    cap = slots // n_expert
    full = width + META
    n_z = n_expert // 2
    dests = slots // (cap * STRIDE)
    per = STRIDE * cap
    down_rows = down_weight.shape[1]
    part = both * META // width
    axes = ("dp", "expert")

    apart = [
        [d * n_expert + (rho + STRIDE * k) * 2 + h for k in range(n_z // STRIDE)]
        for d in range(n_dp)
        for rho in range(STRIDE)
        for h in range(2)
    ]
    near = [
        [
            d * n_expert + ((STRIDE * a + (rho - 2 * (d % 2)) % STRIDE + 2 * (d % 2)) % n_z) * 2 + h
            for rho in range(STRIDE)
            for h in range(2)
        ]
        for d in range(n_dp)
        for a in range(n_z // STRIDE)
    ]
    core, me = lax.axis_index("dp") % 2, lax.axis_index("expert")
    shift = 2 * core
    quad = ((me // 2 - shift + n_z) % n_z) // STRIDE
    rho = jnp.arange(dests, dtype=jnp.int32) // 2
    members = ((STRIDE * quad + (rho - shift + STRIDE) % STRIDE + shift) % n_z) * 2 + jnp.arange(
        dests, dtype=jnp.int32
    ) % 2
    mine = me.reshape(1).astype(jnp.int32)

    rows, pack = pl.pallas_call(
        prep_kernel,
        out_shape=(shape((tok, full)), shape((part + down_rows, width))),
        in_specs=[whole()] * 6,
        out_specs=(whole(), whole()),
        compiler_params=params(),
        name="prep",
    )(grad_out, expert_ids, route_weights, gate_weight[0], up_weight[0], down_weight[0])
    packs = lax.all_gather(pack, "dp", axis=0, tiled=False)
    blocks = lax.all_gather(rows, axes, axis=0, tiled=True, axis_index_groups=apart)
    send, select = pl.pallas_call(
        functools.partial(select_kernel, cap),
        out_shape=(shape((dests, per, full)), shape((slots, STRIDE * tok))),
        in_specs=[whole(pltpu.SMEM), whole()],
        out_specs=(whole(), whole()),
        compiler_params=params(),
        name="select",
    )(members, blocks)
    got = lax.all_to_all(send, axes, 0, 0, axis_index_groups=near, tiled=True).reshape(slots, full)
    hid, turned, slope, silu = pl.pallas_call(
        functools.partial(act_kernel, cap),
        out_shape=(
            shape((slots, hidden)),
            shape((hidden, slots)),
            shape((slots, hidden), F32),
            shape((slots, hidden), F32),
        ),
        in_specs=[whole()],
        out_specs=(whole(),) * 4,
        compiler_params=params(),
        cost_estimate=pl.CostEstimate(flops=slots * slots * both * 2, bytes_accessed=8 * slots * both, transcendentals=0),
        name="act",
    )(pre)
    columns = 512
    down_part = pl.pallas_call(
        down_kernel,
        out_shape=shape((hidden, width)),
        grid=(width // columns,),
        in_specs=[
            whole(pltpu.SMEM),
            pl.BlockSpec((slots, columns), lambda i: (0, i)),
            pl.BlockSpec((slots, META), lambda i: (0, width // META)),
            pl.BlockSpec((hidden, slots), lambda i: (0, 0)),
        ],
        out_specs=pl.BlockSpec((hidden, columns), lambda i: (0, i)),
        compiler_params=params(),
        cost_estimate=pl.CostEstimate(flops=2 * slots * hidden * width, bytes_accessed=2 * (slots + hidden) * width, transcendentals=0),
        name="down",
    )(mine, got, got, turned)
    down_grad = lax.psum_scatter(down_part, "dp", scatter_dimension=0, tiled=True)
    pair = 2
    back = pl.pallas_call(
        mid_kernel,
        out_shape=shape((slots, full)),
        grid=(1 + n_dp // pair,),
        in_specs=[
            whole(pltpu.SMEM),
            pl.BlockSpec((slots, full), lambda i: (0, 0)),
            pl.BlockSpec((slots, hidden), lambda i: (0, 0)),
            pl.BlockSpec((slots, hidden), lambda i: (0, 0)),
            pl.BlockSpec((slots, hidden), lambda i: (0, 0)),
            pl.BlockSpec((n_dp, down_rows, width), lambda i: (0, part // down_rows, 0)),
            pl.BlockSpec((pair, part, width), lambda i: (jnp.maximum(i - 1, 0), 0, 0)),
        ],
        out_specs=pl.BlockSpec((slots, full), lambda i: (0, 0)),
        scratch_shapes=[pltpu.VMEM((slots, both), BF16), pltpu.VMEM((both, pair * META), BF16)],
        compiler_params=params(),
        cost_estimate=pl.CostEstimate(flops=6 * slots * hidden * width, bytes_accessed=2 * 3 * hidden * width, transcendentals=0),
        name="mid",
    )(mine, got, hid, slope, silu, packs, packs)
    back = lax.all_to_all(
        back.reshape(dests, per, full), axes, 0, 0, axis_index_groups=near, tiled=True
    ).reshape(slots, full)
    partial = pl.pallas_call(
        combine_kernel,
        out_shape=shape((STRIDE * tok, full)),
        in_specs=[whole(), whole()],
        out_specs=whole(),
        compiler_params=params(),
        name="combine",
    )(select, back)
    parts = lax.all_to_all(
        partial.reshape(STRIDE, tok, full), axes, 0, 0, axis_index_groups=apart, tiled=True
    )
    token_grad, route_grad = pl.pallas_call(
        last_kernel,
        out_shape=(shape((tok, width)), shape(expert_ids.shape)),
        in_specs=[whole(), whole()],
        out_specs=(whole(), whole()),
        compiler_params=params(),
        name="last",
    )(parts, expert_ids)
    return token_grad, route_grad, down_grad[None]


def solution(mesh):
    return jax.shard_map(
        functools.partial(per_device, mesh.shape["dp"], mesh.shape["expert"]),
        mesh=mesh,
        in_specs=(
            P(("dp", "expert"), None),
            P(("dp", "expert"), None),
            P(("dp", "expert"), None),
            P("dp", "expert", None, None),
            P("expert", "dp", None),
            P("expert", "dp", None),
            P("expert", "dp", None),
        ),
        out_specs=(P(("dp", "expert"), None), P(("dp", "expert"), None), P("expert", "dp", None)),
        check_vma=False,
    )
```

```python
import functools

import jax
import jax.numpy as jnp
from jax import lax
from jax.experimental import pallas as pl
from jax.experimental.pallas import tpu as pltpu
from jax.sharding import PartitionSpec as P

BF16, F32 = jnp.bfloat16, jnp.float32
META = 128
STRIDE = 4


def params(mib):
    return pltpu.CompilerParams(vmem_limit_bytes=mib * 1024 * 1024)


def turn(values):
    rows, columns = values.shape
    if columns < META:
        values = jnp.concatenate([values, jnp.zeros((rows, META - columns), F32)], axis=1)
    if rows < META:
        values = jnp.concatenate([values, jnp.zeros((META - rows, META), F32)], axis=0)
    return values.T[:columns, :rows] if columns < META else values.T[:, :rows]


def prep_kernel(
    rows_ref, ids_ref, weight_ref, gate_ref, up_ref, down_ref, tok_ref, pack_ref,
    ids_buf, weight_buf, gate_buf, up_buf, sems,
):
    tok, width = rows_ref.shape
    topk = ids_ref.shape[0]
    hidden = gate_ref.shape[1]
    part = 2 * hidden * META // width
    copies = [
        pltpu.make_async_copy(gate_ref, gate_buf, sems.at[0]),
        pltpu.make_async_copy(up_ref, up_buf, sems.at[1]),
        pltpu.make_async_copy(down_ref, pack_ref.at[pl.ds(part, down_ref.shape[0]), :], sems.at[2]),
        pltpu.make_async_copy(ids_ref, ids_buf, sems.at[3]),
        pltpu.make_async_copy(weight_ref, weight_buf, sems.at[4]),
        pltpu.make_async_copy(rows_ref, tok_ref.at[:, pl.ds(0, width)], sems.at[5]),
    ]
    for copy in copies:
        copy.start()
    for at, buf in enumerate((gate_buf, up_buf)):
        copies[at].wait()
        turned = buf[...].astype(F32).T.astype(BF16)
        for g in range(hidden // part):
            lane = (at * (hidden // part) + g) * META
            pack_ref[0:part, lane : lane + META] = turned[g * part : (g + 1) * part]
    copies[3].wait()
    copies[4].wait()
    meta = jnp.concatenate([ids_buf[...].astype(F32), weight_buf[...].astype(F32)], axis=0)
    meta = jnp.concatenate([meta, jnp.zeros((META - 2 * topk, tok), F32)], axis=0)
    tok_ref[:, width:] = turn(meta).astype(BF16)
    copies[2].wait()
    copies[5].wait()


def select_kernel(cap, mine_ref, tok_ref, send_ref, select_ref):
    rows, full = tok_ref.shape
    width = full - META
    dests, per, _ = send_ref.shape
    block = rows // STRIDE
    topk = 8
    ids = tok_ref[:, width:].astype(F32).T[0:topk, :]
    member = jnp.concatenate(
        [
            jnp.max((ids == mine_ref[j].astype(F32)).astype(F32), axis=0, keepdims=True)
            for j in range(dests)
        ],
        axis=0,
    )
    before = lax.broadcasted_iota(jnp.int32, (rows, rows), 0)
    after = lax.broadcasted_iota(jnp.int32, (rows, rows), 1)
    earlier = (before < after) & (before // block == after // block)
    rank = jnp.dot(member.astype(BF16), earlier.astype(BF16), preferred_element_type=F32)
    key = jnp.where(member > 0.0, rank, -1.0)
    place = lax.broadcasted_iota(jnp.int32, (per, rows), 0)
    source = lax.broadcasted_iota(jnp.int32, (per, rows), 1) // block
    pattern = jnp.where(place // cap == source, place - source * cap, -2).astype(F32)
    for j in range(dests):
        chosen = (key[j : j + 1, :] == pattern).astype(BF16)
        select_ref[j * per : (j + 1) * per, :] = chosen
    for j in range(dests):
        send_ref[j] = jnp.dot(
            select_ref[j * per : (j + 1) * per, :], tok_ref[...], preferred_element_type=F32
        ).astype(BF16)


def act_kernel(cap, rows, pre_ref, hid_ref, turned_ref, slope_ref, silu_ref):
    slots, both = pre_ref.shape
    hidden = both // 2
    dests = slots // (cap * STRIDE)
    at = lax.broadcasted_iota(jnp.int32, (slots, slots), 0)
    src = lax.broadcasted_iota(jnp.int32, (slots, slots), 1)
    j, rest = at // (STRIDE * cap), at % (STRIDE * cap)
    k, r = rest // cap, rest % cap
    order = (src == (k * dests + j) * cap + r).astype(BF16)
    a = jnp.dot(order, pre_ref[:, :hidden], preferred_element_type=F32)
    u = jnp.dot(order, pre_ref[:, hidden:], preferred_element_type=F32)
    sig = jax.nn.sigmoid(a)
    silu = a * sig
    hid = (silu * u).astype(BF16)
    hid_ref[...] = hid
    turned = hid.astype(F32).T.astype(BF16)
    for block in range(hidden // rows):
        at = (block % 2) * (hidden // 2) + (block // 2) * rows
        turned_ref[at : at + rows, :] = turned[block * rows : (block + 1) * rows]
    slope_ref[...] = u * sig * (1.0 + a * (1.0 - sig))
    silu_ref[...] = silu


def slot_weight(meta, expert):
    topk = 8
    meta = meta.astype(F32)
    lane = lax.broadcasted_iota(jnp.int32, meta.shape, 1)
    weight = pltpu.roll(meta, META - topk, 1)
    return jnp.sum(jnp.where((lane < topk) & (meta == expert.astype(F32)), weight, 0.0), axis=1, keepdims=True)


def down_kernel(mine_ref, got_ref, turned_ref, keep_ref, send_ref):
    half, width = keep_ref.shape
    core = mine_ref[1]
    w = slot_weight(got_ref[:, width:], mine_ref[0])
    columns = 512
    for at in range(0, width, columns):
        scaled = (w * got_ref[:, at : at + columns].astype(F32)).astype(BF16)
        for ref, which in ((send_ref, 1 - core), (keep_ref, core)):
            begin = pl.multiple_of(which * half, half)
            ref[:, at : at + columns] = jnp.dot(
                turned_ref[pl.ds(begin, half), :], scaled, preferred_element_type=F32
            ).astype(BF16)


def mid_kernel(
    mine_ref, got_ref, hid_ref, slope_ref, silu_ref, pack_ref, out_ref,
    out_buf, both_buf, down_buf, pack_buf, wide_buf, in_sems, out_sems,
):
    width = got_ref.shape[1] - META
    hidden = hid_ref.shape[1]
    pairs, pair, part, _ = pack_buf.shape
    down_rows = down_buf.shape[1]
    down_copy = pltpu.make_async_copy(
        pack_ref.at[:, pl.ds(part, down_rows), :], down_buf, in_sems.at[pairs]
    )
    down_copy.start()
    copies = [
        pltpu.make_async_copy(
            pack_ref.at[pl.ds(p * pair, pair), pl.ds(0, part), :], pack_buf.at[p], in_sems.at[p]
        )
        for p in range(pairs)
    ]
    for copy in copies:
        copy.start()
    w = slot_weight(got_ref[:, width:], mine_ref[0])
    down_copy.wait()
    q = lax.dot_general(
        got_ref[:, :width],
        down_buf[...].reshape(hidden, width),
        (((1,), (1,)), ((), ())),
        preferred_element_type=F32,
    )
    route = jnp.sum(q * hid_ref[...].astype(F32), axis=1, keepdims=True)
    grad = w * q
    both_buf[:, :hidden] = (grad * slope_ref[...]).astype(BF16)
    both_buf[:, hidden:] = (grad * silu_ref[...]).astype(BF16)
    lane = lax.broadcasted_iota(jnp.int32, (got_ref.shape[0], META), 1)
    out_buf[:, width:] = jnp.where(lane == mine_ref[0], route, 0.0).astype(BF16)
    backs = [pltpu.make_async_copy(out_buf.at[:, pl.ds(width, META)], out_ref.at[:, pl.ds(width, META)], out_sems.at[pairs])]
    backs[0].start()
    for p in range(pairs):
        copies[p].wait()
        for b in range(pair):
            for g in range(2 * hidden // part):
                wide_buf[p % 2, g * part : (g + 1) * part, b * META : (b + 1) * META] = pack_buf[
                    p, b, :, g * META : (g + 1) * META
                ]
        at = p * pair * META
        out_buf[:, at : at + pair * META] = jnp.dot(
            both_buf[...], wide_buf[p % 2], preferred_element_type=F32
        ).astype(BF16)
        columns = pl.ds(at, pair * META)
        backs.append(pltpu.make_async_copy(out_buf.at[:, columns], out_ref.at[:, columns], out_sems.at[p]))
        backs[-1].start()
    for copy in backs:
        copy.wait()


def combine_kernel(place_ref, select_ref, back_ref, *refs):
    outs, total_buf = refs[:-1], refs[-1]
    tok = outs[0].shape[0]
    total_buf[...] = lax.dot_general(
        select_ref[...], back_ref[...], (((0,), (0,)), ((), ())), preferred_element_type=F32
    )
    for m, ref in enumerate(outs):
        begin = pl.multiple_of(((place_ref[0] + m) % STRIDE) * tok, tok)
        ref[...] = total_buf[pl.ds(begin, tok), :].astype(ref.dtype)


def last_kernel(ids_ref, *refs):
    parts, (tok_ref, route_ref) = refs[:STRIDE], refs[STRIDE:]
    tok, width = tok_ref.shape
    total = parts[0][...]
    for ref in parts[1:]:
        total = total + ref[...].astype(F32)
    tok_ref[...] = total[:, :width].astype(BF16)
    route = turn(total[:, width:])
    ids = ids_ref[...]
    expert = lax.broadcasted_iota(jnp.int32, route.shape, 0)
    found = [
        jnp.sum(jnp.where(expert == ids[k : k + 1, :], route, 0.0), axis=0, keepdims=True)
        for k in range(ids.shape[0])
    ]
    route_ref[...] = jnp.concatenate(found, axis=0).astype(BF16)


def shape(dims, dtype=BF16):
    return jax.ShapeDtypeStruct(dims, dtype)


def whole(memory=pltpu.VMEM):
    return pl.BlockSpec(memory_space=memory)


def per_device(n_dp, n_expert, grad_out, expert_ids, route_weights, saved_pre, gate_weight, up_weight, down_weight):
    tok, width = grad_out.shape
    pre = saved_pre[0, 0]
    slots, both = pre.shape
    hidden = both // 2
    cap = slots // n_expert
    full = width + META
    n_z = n_expert // 2
    dests = slots // (cap * STRIDE)
    per = STRIDE * cap
    down_rows = down_weight.shape[1]
    part = both * META // width
    axes = ("dp", "expert")

    apart = [
        [d * n_expert + (rho + STRIDE * k) * 2 + h for k in range(n_z // STRIDE)]
        for d in range(n_dp)
        for rho in range(STRIDE)
        for h in range(2)
    ]
    near = [
        [
            d * n_expert + ((STRIDE * a + (rho - 2 * (d % 2)) % STRIDE + 2 * (d % 2)) % n_z) * 2 + h
            for rho in range(STRIDE)
            for h in range(2)
        ]
        for d in range(n_dp)
        for a in range(n_z // STRIDE)
    ]
    core, me = lax.axis_index("dp") % 2, lax.axis_index("expert")
    shift = 2 * core
    quad = ((me // 2 - shift + n_z) % n_z) // STRIDE
    rho = jnp.arange(dests, dtype=jnp.int32) // 2
    members = ((STRIDE * quad + (rho - shift + STRIDE) % STRIDE + shift) % n_z) * 2 + jnp.arange(
        dests, dtype=jnp.int32
    ) % 2
    mine = jnp.stack([me, core]).astype(jnp.int32)

    rows, pack = pl.pallas_call(
        prep_kernel,
        out_shape=(shape((tok, full)), shape((part + down_rows, width))),
        in_specs=[whole(pltpu.HBM)] * 6,
        out_specs=(whole(), whole()),
        scratch_shapes=[
            pltpu.VMEM((expert_ids.shape[1], tok), jnp.int32),
            pltpu.VMEM((expert_ids.shape[1], tok), BF16),
            pltpu.VMEM((META, hidden), BF16),
            pltpu.VMEM((META, hidden), BF16),
            pltpu.SemaphoreType.DMA((6,)),
        ],
        compiler_params=params(12),
        name="prep",
    )(grad_out, expert_ids.T, route_weights.T, gate_weight[0], up_weight[0], down_weight[0])
    packs = lax.all_gather(pack, "dp", axis=0, tiled=False)
    blocks = lax.all_gather(rows, axes, axis=0, tiled=True, axis_index_groups=apart)
    send, select = pl.pallas_call(
        functools.partial(select_kernel, cap),
        out_shape=(shape((dests, per, full)), shape((slots, STRIDE * tok))),
        in_specs=[whole(pltpu.SMEM), whole()],
        out_specs=(whole(), whole()),
        compiler_params=params(16),
        name="select",
    )(members, blocks)
    got = lax.all_to_all(send, axes, 0, 0, axis_index_groups=near, tiled=True).reshape(slots, full)
    hid, turned, slope, silu = pl.pallas_call(
        functools.partial(act_kernel, cap, down_rows),
        out_shape=(
            shape((slots, hidden)),
            shape((hidden, slots)),
            shape((slots, hidden), F32),
            shape((slots, hidden), F32),
        ),
        in_specs=[whole()],
        out_specs=(whole(),) * 4,
        compiler_params=params(24),
        cost_estimate=pl.CostEstimate(flops=slots * slots * both * 2, bytes_accessed=8 * slots * both, transcendentals=0),
        name="act",
    )(pre)
    keep, give = pl.pallas_call(
        down_kernel,
        out_shape=(shape((hidden // 2, width)), shape((hidden // 2, width))),
        in_specs=[whole(pltpu.SMEM), whole(), whole()],
        out_specs=(whole(), whole()),
        compiler_params=params(20),
        cost_estimate=pl.CostEstimate(flops=2 * slots * hidden * width, bytes_accessed=2 * (slots + hidden) * width, transcendentals=0),
        name="down",
    )(mine, got, turned)
    taken = lax.ppermute(give, "dp", [(d, d ^ 1) for d in range(n_dp)])
    chip_part = (keep.astype(F32) + taken.astype(F32)).astype(BF16)
    got, chip_part = lax.optimization_barrier((got, chip_part))
    down_grad = lax.psum_scatter(
        chip_part,
        "dp",
        scatter_dimension=0,
        tiled=True,
        axis_index_groups=[list(range(c, n_dp, 2)) for c in range(2)],
    )
    pair = 2
    back = pl.pallas_call(
        mid_kernel,
        out_shape=shape((slots, full)),
        in_specs=[whole(pltpu.SMEM)] + [whole()] * 4 + [whole(pltpu.HBM)],
        out_specs=whole(pltpu.HBM),
        scratch_shapes=[
            pltpu.VMEM((slots, full), BF16),
            pltpu.VMEM((slots, both), BF16),
            pltpu.VMEM((n_dp, down_rows, width), BF16),
            pltpu.VMEM((n_dp // pair, pair, part, width), BF16),
            pltpu.VMEM((2, both, pair * META), BF16),
            pltpu.SemaphoreType.DMA((n_dp // pair + 1,)),
            pltpu.SemaphoreType.DMA((n_dp // pair + 1,)),
        ],
        compiler_params=params(36),
        cost_estimate=pl.CostEstimate(flops=6 * slots * hidden * width, bytes_accessed=2 * 3 * hidden * width, transcendentals=0),
        name="mid",
    )(mine, got, hid, slope, silu, packs)
    back = lax.all_to_all(
        back.reshape(dests, per, full), axes, 0, 0, axis_index_groups=near, tiled=True
    ).reshape(slots, full)
    place = (me // 2 // STRIDE).reshape(1).astype(jnp.int32)
    own, *sums = pl.pallas_call(
        combine_kernel,
        out_shape=(shape((tok, full), F32),) + (shape((tok, full)),) * (STRIDE - 1),
        in_specs=[whole(pltpu.SMEM), whole(), whole()],
        out_specs=(whole(),) * STRIDE,
        scratch_shapes=[pltpu.VMEM((STRIDE * tok, full), F32)],
        compiler_params=params(12),
        name="combine",
    )(place, select, back)
    parts = [own] + [
        lax.ppermute(
            value,
            "expert",
            [(e, ((e // 2 + STRIDE * (m + 1)) % n_z) * 2 + e % 2) for e in range(n_expert)],
        )
        for m, value in enumerate(sums)
    ]
    token_grad, route_grad = pl.pallas_call(
        last_kernel,
        out_shape=(shape((tok, width)), shape(expert_ids.shape[::-1])),
        in_specs=[whole()] * (1 + STRIDE),
        out_specs=(whole(), whole()),
        compiler_params=params(8),
        name="last",
    )(expert_ids.T, *parts)
    return token_grad, route_grad.T, down_grad[None]


def solution(mesh):
    return jax.shard_map(
        functools.partial(per_device, mesh.shape["dp"], mesh.shape["expert"]),
        mesh=mesh,
        in_specs=(
            P(("dp", "expert"), None),
            P(("dp", "expert"), None),
            P(("dp", "expert"), None),
            P("dp", "expert", None, None),
            P("expert", "dp", None),
            P("expert", "dp", None),
            P("expert", "dp", None),
        ),
        out_specs=(P(("dp", "expert"), None), P(("dp", "expert"), None), P("expert", "dp", None)),
        check_vma=False,
    )
```

```python
import functools

import jax
import jax.numpy as jnp
from jax import lax
from jax.experimental import pallas as pl
from jax.experimental.pallas import tpu as pltpu
from jax.sharding import PartitionSpec as P

BF16, F32 = jnp.bfloat16, jnp.float32
META = 128
TILE = 512
STRIDE = 4


def params(mib):
    return pltpu.CompilerParams(vmem_limit_bytes=mib * 1024 * 1024)


def turn(values):
    rows, columns = values.shape
    if columns < META:
        values = jnp.concatenate([values, jnp.zeros((rows, META - columns), F32)], axis=1)
    if rows < META:
        values = jnp.concatenate([values, jnp.zeros((META - rows, META), F32)], axis=0)
    return values.T[:columns, :rows] if columns < META else values.T[:, :rows]


def prep_kernel(
    rows_ref, ids_ref, weight_ref, gate_ref, up_ref, down_ref, tok_ref, first_ref, second_ref,
    ids_buf, weight_buf, gate_buf, up_buf, sems,
):
    tok, width = rows_ref.shape
    topk = ids_ref.shape[0]
    hidden = gate_ref.shape[1]
    down_rows = down_ref.shape[0]
    copies = [
        pltpu.make_async_copy(gate_ref, gate_buf, sems.at[0]),
        pltpu.make_async_copy(up_ref, up_buf, sems.at[1]),
        pltpu.make_async_copy(down_ref, first_ref.at[pl.ds(0, down_rows), :], sems.at[2]),
        pltpu.make_async_copy(ids_ref, ids_buf, sems.at[3]),
        pltpu.make_async_copy(weight_ref, weight_buf, sems.at[4]),
        pltpu.make_async_copy(rows_ref, tok_ref.at[:, pl.ds(0, width)], sems.at[5]),
    ]
    for copy in copies:
        copy.start()
    copies[0].wait()
    copies[1].wait()
    piece = TILE // 2
    half = gate_ref.shape[0] // 2
    for which, (ref, base) in enumerate(((first_ref, down_rows), (second_ref, 0))):
        for i in range(half // 16):
            for p in range(2 * hidden // piece):
                n = i * (2 * hidden // TILE) + p // 2
                row = base + n // (width // TILE) * 16
                lane = n % (width // TILE) * TILE + p % 2 * piece
                buf = gate_buf if p * piece < hidden else up_buf
                src = p * piece % hidden
                begin = which * half + i * 16
                ref[row : row + 16, lane : lane + piece] = buf[begin : begin + 16, src : src + piece]
    copies[3].wait()
    copies[4].wait()
    meta = jnp.concatenate([ids_buf[...].astype(F32), weight_buf[...].astype(F32)], axis=0)
    meta = jnp.concatenate([meta, jnp.zeros((META - 2 * topk, tok), F32)], axis=0)
    tok_ref[:, width:] = turn(meta).astype(BF16)
    copies[2].wait()
    copies[5].wait()


def select_kernel(cap, mine_ref, tok_ref, send_ref, select_ref):
    rows, full = tok_ref.shape
    width = full - META
    dests, per, _ = send_ref.shape
    block = rows // STRIDE
    topk = 8
    ids = tok_ref[:, width:].astype(F32).T[0:topk, :]
    member = jnp.concatenate(
        [
            jnp.max((ids == mine_ref[j].astype(F32)).astype(F32), axis=0, keepdims=True)
            for j in range(dests)
        ],
        axis=0,
    )
    before = lax.broadcasted_iota(jnp.int32, (rows, rows), 0)
    after = lax.broadcasted_iota(jnp.int32, (rows, rows), 1)
    earlier = (before < after) & (before // block == after // block)
    rank = jnp.dot(member.astype(BF16), earlier.astype(BF16), preferred_element_type=F32)
    key = jnp.where(member > 0.0, rank, -1.0)
    place = lax.broadcasted_iota(jnp.int32, (per, rows), 0)
    source = lax.broadcasted_iota(jnp.int32, (per, rows), 1) // block
    pattern = jnp.where(place // cap == source, place - source * cap, -2).astype(F32)
    for j in range(dests):
        chosen = (key[j : j + 1, :] == pattern).astype(BF16)
        select_ref[j * per : (j + 1) * per, :] = chosen
    for j in range(dests):
        send_ref[j] = jnp.dot(
            select_ref[j * per : (j + 1) * per, :], tok_ref[...], preferred_element_type=F32
        ).astype(BF16)


def act_kernel(cap, rows, pre_ref, hid_ref, turned_ref, slope_ref, silu_ref):
    slots, both = pre_ref.shape
    hidden = both // 2
    dests = slots // (cap * STRIDE)
    at = lax.broadcasted_iota(jnp.int32, (slots, slots), 0)
    src = lax.broadcasted_iota(jnp.int32, (slots, slots), 1)
    j, rest = at // (STRIDE * cap), at % (STRIDE * cap)
    k, r = rest // cap, rest % cap
    order = (src == (k * dests + j) * cap + r).astype(BF16)
    a = jnp.dot(order, pre_ref[:, :hidden], preferred_element_type=F32)
    u = jnp.dot(order, pre_ref[:, hidden:], preferred_element_type=F32)
    sig = jax.nn.sigmoid(a)
    silu = a * sig
    hid = (silu * u).astype(BF16)
    hid_ref[...] = hid
    turned = hid.astype(F32).T.astype(BF16)
    for block in range(hidden // rows):
        at = (block % 2) * (hidden // 2) + (block // 2) * rows
        turned_ref[at : at + rows, :] = turned[block * rows : (block + 1) * rows]
    slope_ref[...] = u * sig * (1.0 + a * (1.0 - sig))
    silu_ref[...] = silu


def slot_weight(meta, expert):
    topk = 8
    meta = meta.astype(F32)
    lane = lax.broadcasted_iota(jnp.int32, meta.shape, 1)
    weight = pltpu.roll(meta, META - topk, 1)
    return jnp.sum(jnp.where((lane < topk) & (meta == expert.astype(F32)), weight, 0.0), axis=1, keepdims=True)


def down_kernel(mine_ref, got_ref, turned_ref, keep_ref, send_ref):
    half, width = keep_ref.shape
    core = mine_ref[1]
    w = slot_weight(got_ref[:, width:], mine_ref[0])
    columns = 512
    for at in range(0, width, columns):
        scaled = (w * got_ref[:, at : at + columns].astype(F32)).astype(BF16)
        for ref, which in ((send_ref, 1 - core), (keep_ref, core)):
            begin = pl.multiple_of(which * half, half)
            ref[:, at : at + columns] = jnp.dot(
                turned_ref[pl.ds(begin, half), :], scaled, preferred_element_type=F32
            ).astype(BF16)


def fetch(pack_ref, base, wide_buf, sems, first):
    _, rows, both = wide_buf.shape
    across, per = both // TILE, pack_ref.shape[2] // TILE
    copies = []
    for i in range(rows // 16):
        for j in range(across):
            n = i * across + j
            copies.append(
                pltpu.make_async_copy(
                    pack_ref.at[:, pl.ds(base + n // per * 16, 16), pl.ds(n % per * TILE, TILE)],
                    wide_buf.at[:, pl.ds(i * 16, 16), pl.ds(j * TILE, TILE)],
                    sems.at[first + n],
                )
            )
    for copy in copies:
        copy.start()
    return copies


def multiply(both_ref, wide_buf, out_buf, out_ref, sems, backs):
    columns = 256
    devices, rows, both = wide_buf.shape
    group = columns // rows
    for n in range(devices // group):
        at = n * columns
        out_buf[:, at : at + columns] = lax.dot_general(
            both_ref[...],
            wide_buf[n * group : (n + 1) * group].reshape(columns, both),
            (((1,), (1,)), ((), ())),
            preferred_element_type=F32,
        ).astype(BF16)
        part = pl.ds(at, columns)
        backs.append(pltpu.make_async_copy(out_buf.at[:, part], out_ref.at[:, part], sems.at[n]))
        backs[-1].start()
    for copy in backs:
        copy.wait()


def first_kernel(
    mine_ref, got_ref, hid_ref, slope_ref, silu_ref, pack_ref, out_ref, both_ref,
    out_buf, down_buf, wide_buf, in_sems, out_sems,
):
    width = got_ref.shape[1] - META
    hidden = hid_ref.shape[1]
    down_rows = down_buf.shape[1]
    half = out_buf.shape[1] - META
    down_copy = pltpu.make_async_copy(pack_ref.at[:, pl.ds(0, down_rows), :], down_buf, in_sems.at[0])
    down_copy.start()
    copies = fetch(pack_ref, down_rows, wide_buf, in_sems, 1)
    w = slot_weight(got_ref[:, width:], mine_ref[0])
    down_copy.wait()
    q = lax.dot_general(
        got_ref[:, :width],
        down_buf[...].reshape(hidden, width),
        (((1,), (1,)), ((), ())),
        preferred_element_type=F32,
    )
    route = jnp.sum(q * hid_ref[...].astype(F32), axis=1, keepdims=True)
    grad = w * q
    both_ref[:, :hidden] = (grad * slope_ref[...]).astype(BF16)
    both_ref[:, hidden:] = (grad * silu_ref[...]).astype(BF16)
    lane = lax.broadcasted_iota(jnp.int32, (got_ref.shape[0], META), 1)
    out_buf[:, half:] = jnp.where(lane == mine_ref[0], route, 0.0).astype(BF16)
    extra = pl.ds(half, META)
    last = out_sems.shape[0] - 1
    backs = [pltpu.make_async_copy(out_buf.at[:, extra], out_ref.at[:, extra], out_sems.at[last])]
    backs[0].start()
    for copy in copies:
        copy.wait()
    multiply(both_ref, wide_buf, out_buf, out_ref, out_sems, backs)


def second_kernel(both_ref, pack_ref, out_ref, out_buf, wide_buf, in_sems, out_sems):
    for copy in fetch(pack_ref, 0, wide_buf, in_sems, 0):
        copy.wait()
    multiply(both_ref, wide_buf, out_buf, out_ref, out_sems, [])


def combine_kernel(place_ref, select_ref, back_ref, *refs):
    outs, total_buf = refs[:-1], refs[-1]
    tok = outs[0].shape[0]
    total_buf[...] = lax.dot_general(
        select_ref[...], back_ref[...], (((0,), (0,)), ((), ())), preferred_element_type=F32
    )
    for m, ref in enumerate(outs):
        begin = pl.multiple_of(((place_ref[0] + m) % STRIDE) * tok, tok)
        ref[...] = total_buf[pl.ds(begin, tok), :].astype(ref.dtype)


def last_kernel(ids_ref, *refs):
    first, second, (tok_ref, route_ref) = refs[:STRIDE], refs[STRIDE : 2 * STRIDE], refs[2 * STRIDE :]
    tok, width = tok_ref.shape
    sums = []
    for parts in (first, second):
        total = parts[0][...]
        for ref in parts[1:]:
            total = total + ref[...].astype(F32)
        sums.append(total)
    low = lax.broadcasted_iota(jnp.int32, (tok, META), 1) < META // 2
    for j in range(width // META // 2):
        a, b = (x[:, j * META : (j + 1) * META] for x in sums)
        tok_ref[:, 2 * j * META : (2 * j + 1) * META] = jnp.where(low, a, pltpu.roll(b, META // 2, 1)).astype(BF16)
        tok_ref[:, (2 * j + 1) * META : (2 * j + 2) * META] = jnp.where(low, pltpu.roll(a, META // 2, 1), b).astype(BF16)
    route = turn(sums[0][:, width // 2 :])
    ids = ids_ref[...]
    expert = lax.broadcasted_iota(jnp.int32, route.shape, 0)
    found = [
        jnp.sum(jnp.where(expert == ids[k : k + 1, :], route, 0.0), axis=0, keepdims=True)
        for k in range(ids.shape[0])
    ]
    route_ref[...] = jnp.concatenate(found, axis=0).astype(BF16)


def shape(dims, dtype=BF16):
    return jax.ShapeDtypeStruct(dims, dtype)


def whole(memory=pltpu.VMEM):
    return pl.BlockSpec(memory_space=memory)


def exchange(value, axes, groups):
    return lax.all_to_all(value, axes, 0, 0, axis_index_groups=groups, tiled=True)


def per_device(n_dp, n_expert, grad_out, expert_ids, route_weights, saved_pre, gate_weight, up_weight, down_weight):
    tok, width = grad_out.shape
    pre = saved_pre[0, 0]
    slots, both = pre.shape
    hidden = both // 2
    cap = slots // n_expert
    full = width + META
    n_z = n_expert // 2
    dests = slots // (cap * STRIDE)
    per = STRIDE * cap
    down_rows = down_weight.shape[1]
    axes = ("dp", "expert")

    apart = [
        [d * n_expert + (rho + STRIDE * k) * 2 + h for k in range(n_z // STRIDE)]
        for d in range(n_dp)
        for rho in range(STRIDE)
        for h in range(2)
    ]
    near = [
        [
            d * n_expert + ((STRIDE * a + (rho - 2 * (d % 2)) % STRIDE + 2 * (d % 2)) % n_z) * 2 + h
            for rho in range(STRIDE)
            for h in range(2)
        ]
        for d in range(n_dp)
        for a in range(n_z // STRIDE)
    ]
    core, me = lax.axis_index("dp") % 2, lax.axis_index("expert")
    shift = 2 * core
    quad = ((me // 2 - shift + n_z) % n_z) // STRIDE
    rho = jnp.arange(dests, dtype=jnp.int32) // 2
    members = ((STRIDE * quad + (rho - shift + STRIDE) % STRIDE + shift) % n_z) * 2 + jnp.arange(
        dests, dtype=jnp.int32
    ) % 2
    mine = jnp.stack([me, core]).astype(jnp.int32)

    half_rows = gate_weight.shape[1] // 2
    part = half_rows * both // width
    rows, pack, pack_b = pl.pallas_call(
        prep_kernel,
        out_shape=(shape((tok, full)), shape((down_rows + part, width)), shape((part, width))),
        in_specs=[whole(pltpu.HBM)] * 6,
        out_specs=(whole(),) * 3,
        scratch_shapes=[
            pltpu.VMEM((expert_ids.shape[1], tok), jnp.int32),
            pltpu.VMEM((expert_ids.shape[1], tok), BF16),
            pltpu.VMEM((2 * half_rows, hidden), BF16),
            pltpu.VMEM((2 * half_rows, hidden), BF16),
            pltpu.SemaphoreType.DMA((6,)),
        ],
        compiler_params=params(60),
        name="prep",
    )(grad_out, expert_ids.T, route_weights.T, gate_weight[0], up_weight[0], down_weight[0])
    packs = lax.all_gather(pack, "dp", axis=0, tiled=False)
    packs_b = lax.all_gather(pack_b, "dp", axis=0, tiled=False)
    blocks = lax.all_gather(rows, axes, axis=0, tiled=True, axis_index_groups=apart)
    send, select = pl.pallas_call(
        functools.partial(select_kernel, cap),
        out_shape=(shape((dests, per, full)), shape((slots, STRIDE * tok))),
        in_specs=[whole(pltpu.SMEM), whole()],
        out_specs=(whole(), whole()),
        compiler_params=params(16),
        name="select",
    )(members, blocks)
    got = exchange(send, axes, near).reshape(slots, full)
    hid, turned, slope, silu = pl.pallas_call(
        functools.partial(act_kernel, cap, down_rows),
        out_shape=(
            shape((slots, hidden)),
            shape((hidden, slots)),
            shape((slots, hidden), F32),
            shape((slots, hidden), F32),
        ),
        in_specs=[whole()],
        out_specs=(whole(),) * 4,
        compiler_params=params(24),
        cost_estimate=pl.CostEstimate(flops=slots * slots * both * 2, bytes_accessed=8 * slots * both, transcendentals=0),
        name="act",
    )(pre)
    columns = 256
    pieces = half_rows // 16 * (both // TILE)
    back, grads = pl.pallas_call(
        first_kernel,
        out_shape=(shape((slots, width // 2 + META)), shape((slots, both))),
        in_specs=[whole(pltpu.SMEM)] + [whole()] * 4 + [whole(pltpu.HBM)],
        out_specs=(whole(pltpu.HBM), whole()),
        scratch_shapes=[
            pltpu.VMEM((slots, width // 2 + META), BF16),
            pltpu.VMEM((n_dp, down_rows, width), BF16),
            pltpu.VMEM((n_dp, half_rows, both), BF16),
            pltpu.SemaphoreType.DMA((pieces + 1,)),
            pltpu.SemaphoreType.DMA((width // 2 // columns + 1,)),
        ],
        compiler_params=params(54),
        cost_estimate=pl.CostEstimate(flops=4 * slots * hidden * width, bytes_accessed=4 * hidden * width, transcendentals=0),
        name="first",
    )(mine, got, hid, slope, silu, packs)
    ret = exchange(back.reshape(dests, per, -1), axes, near).reshape(slots, -1)

    got, back = lax.optimization_barrier((got, back))
    keep, give = pl.pallas_call(
        down_kernel,
        out_shape=(shape((hidden // 2, width)), shape((hidden // 2, width))),
        in_specs=[whole(pltpu.SMEM), whole(), whole()],
        out_specs=(whole(), whole()),
        compiler_params=params(20),
        cost_estimate=pl.CostEstimate(flops=2 * slots * hidden * width, bytes_accessed=2 * (slots + hidden) * width, transcendentals=0),
        name="down",
    )(mine, got, turned)
    taken = lax.ppermute(give, "dp", [(d, d ^ 1) for d in range(n_dp)])
    chip_part = (keep.astype(F32) + taken.astype(F32)).astype(BF16)
    down_grad = lax.psum_scatter(
        chip_part,
        "dp",
        scatter_dimension=0,
        tiled=True,
        axis_index_groups=[list(range(c, n_dp, 2)) for c in range(2)],
    )

    back_b = pl.pallas_call(
        second_kernel,
        out_shape=shape((slots, width // 2)),
        in_specs=[whole(), whole(pltpu.HBM)],
        out_specs=whole(pltpu.HBM),
        scratch_shapes=[
            pltpu.VMEM((slots, width // 2), BF16),
            pltpu.VMEM((n_dp, half_rows, both), BF16),
            pltpu.SemaphoreType.DMA((pieces,)),
            pltpu.SemaphoreType.DMA((width // 2 // columns,)),
        ],
        compiler_params=params(56),
        cost_estimate=pl.CostEstimate(flops=2 * slots * hidden * width, bytes_accessed=2 * hidden * width, transcendentals=0),
        name="second",
    )(grads, packs_b)
    ret_b = exchange(back_b.reshape(dests, per, -1), axes, near).reshape(slots, -1)
    ret, back_b = lax.optimization_barrier((ret, back_b))

    place = (me // 2 // STRIDE).reshape(1).astype(jnp.int32)
    parts = []
    for name, value in (("sum_first", ret), ("sum_second", ret_b)):
        dims = (tok, value.shape[1])
        own, *sums = pl.pallas_call(
            combine_kernel,
            out_shape=(shape(dims, F32),) + (shape(dims),) * (STRIDE - 1),
            in_specs=[whole(pltpu.SMEM), whole(), whole()],
            out_specs=(whole(),) * STRIDE,
            scratch_shapes=[pltpu.VMEM((STRIDE * tok, value.shape[1]), F32)],
            compiler_params=params(12),
            name=name,
        )(place, select, value)
        parts.append(own)
        for m, one in enumerate(sums):
            perm = [(e, ((e // 2 + STRIDE * (m + 1)) % n_z) * 2 + e % 2) for e in range(n_expert)]
            parts.append(lax.ppermute(one, "expert", perm))
    token_grad, route_grad = pl.pallas_call(
        last_kernel,
        out_shape=(shape((tok, width)), shape(expert_ids.shape[::-1])),
        in_specs=[whole()] * (1 + 2 * STRIDE),
        out_specs=(whole(), whole()),
        compiler_params=params(8),
        name="last",
    )(expert_ids.T, *parts)
    return token_grad, route_grad.T, down_grad[None]


def solution(mesh):
    return jax.shard_map(
        functools.partial(per_device, mesh.shape["dp"], mesh.shape["expert"]),
        mesh=mesh,
        in_specs=(
            P(("dp", "expert"), None),
            P(("dp", "expert"), None),
            P(("dp", "expert"), None),
            P("dp", "expert", None, None),
            P("expert", "dp", None),
            P("expert", "dp", None),
            P("expert", "dp", None),
        ),
        out_specs=(P(("dp", "expert"), None), P(("dp", "expert"), None), P("expert", "dp", None)),
        check_vma=False,
    )
```

```python
import functools

import jax
import jax.numpy as jnp
from jax import lax
from jax.experimental import pallas as pl
from jax.experimental.pallas import tpu as pltpu
from jax.sharding import PartitionSpec as P

BF16, F32 = jnp.bfloat16, jnp.float32
META = 128
TILE = 512
STRIDE = 4


def params(mib):
    return pltpu.CompilerParams(vmem_limit_bytes=mib * 1024 * 1024)


def turn(values):
    rows, columns = values.shape
    if columns < META:
        values = jnp.concatenate([values, jnp.zeros((rows, META - columns), F32)], axis=1)
    if rows < META:
        values = jnp.concatenate([values, jnp.zeros((META - rows, META), F32)], axis=0)
    return values.T[:columns, :rows] if columns < META else values.T[:, :rows]


def prep_kernel(
    rows_ref, ids_ref, weight_ref, gate_ref, up_ref, down_ref, tok_ref, pack_ref,
    ids_buf, weight_buf, gate_buf, up_buf, sems,
):
    tok, width = rows_ref.shape
    topk = ids_ref.shape[0]
    hidden = gate_ref.shape[1]
    down_rows = down_ref.shape[0]
    copies = [
        pltpu.make_async_copy(gate_ref, gate_buf, sems.at[0]),
        pltpu.make_async_copy(up_ref, up_buf, sems.at[1]),
        pltpu.make_async_copy(down_ref, pack_ref.at[pl.ds(0, down_rows), :], sems.at[2]),
        pltpu.make_async_copy(ids_ref, ids_buf, sems.at[3]),
        pltpu.make_async_copy(weight_ref, weight_buf, sems.at[4]),
        pltpu.make_async_copy(rows_ref, tok_ref.at[:, pl.ds(0, width)], sems.at[5]),
    ]
    for copy in copies:
        copy.start()
    copies[0].wait()
    copies[1].wait()
    piece = TILE // 2
    for i in range(gate_ref.shape[0] // 16):
        for p in range(2 * hidden // piece):
            n = i * (2 * hidden // TILE) + p // 2
            row = down_rows + n // (width // TILE) * 16
            lane = n % (width // TILE) * TILE + p % 2 * piece
            buf = gate_buf if p * piece < hidden else up_buf
            src = p * piece % hidden
            pack_ref[row : row + 16, lane : lane + piece] = buf[i * 16 : i * 16 + 16, src : src + piece]
    copies[3].wait()
    copies[4].wait()
    meta = jnp.concatenate([ids_buf[...].astype(F32), weight_buf[...].astype(F32)], axis=0)
    meta = jnp.concatenate([meta, jnp.zeros((META - 2 * topk, tok), F32)], axis=0)
    tok_ref[:, width:] = turn(meta).astype(BF16)
    copies[2].wait()
    copies[5].wait()


def select_kernel(cap, mine_ref, tok_ref, send_ref, select_ref):
    rows, full = tok_ref.shape
    width = full - META
    dests, per, _ = send_ref.shape
    block = rows // STRIDE
    topk = 8
    ids = tok_ref[:, width:].astype(F32).T[0:topk, :]
    member = jnp.concatenate(
        [
            jnp.max((ids == mine_ref[j].astype(F32)).astype(F32), axis=0, keepdims=True)
            for j in range(dests)
        ],
        axis=0,
    )
    before = lax.broadcasted_iota(jnp.int32, (rows, rows), 0)
    after = lax.broadcasted_iota(jnp.int32, (rows, rows), 1)
    earlier = (before < after) & (before // block == after // block)
    rank = jnp.dot(member.astype(BF16), earlier.astype(BF16), preferred_element_type=F32)
    key = jnp.where(member > 0.0, rank, -1.0)
    place = lax.broadcasted_iota(jnp.int32, (per, rows), 0)
    source = lax.broadcasted_iota(jnp.int32, (per, rows), 1) // block
    pattern = jnp.where(place // cap == source, place - source * cap, -2).astype(F32)
    for j in range(dests):
        chosen = (key[j : j + 1, :] == pattern).astype(BF16)
        select_ref[j * per : (j + 1) * per, :] = chosen
    for j in range(dests):
        send_ref[j] = jnp.dot(
            select_ref[j * per : (j + 1) * per, :], tok_ref[...], preferred_element_type=F32
        ).astype(BF16)


def act_kernel(cap, rows, pre_ref, hid_ref, turned_ref, slope_ref, silu_ref):
    slots, both = pre_ref.shape
    hidden = both // 2
    dests = slots // (cap * STRIDE)
    at = lax.broadcasted_iota(jnp.int32, (slots, slots), 0)
    src = lax.broadcasted_iota(jnp.int32, (slots, slots), 1)
    j, rest = at // (STRIDE * cap), at % (STRIDE * cap)
    k, r = rest // cap, rest % cap
    order = (src == (k * dests + j) * cap + r).astype(BF16)
    a = jnp.dot(order, pre_ref[:, :hidden], preferred_element_type=F32)
    u = jnp.dot(order, pre_ref[:, hidden:], preferred_element_type=F32)
    sig = jax.nn.sigmoid(a)
    silu = a * sig
    hid = (silu * u).astype(BF16)
    hid_ref[...] = hid
    turned = hid.astype(F32).T.astype(BF16)
    for block in range(hidden // rows):
        at = (block % 2) * (hidden // 2) + (block // 2) * rows
        turned_ref[at : at + rows, :] = turned[block * rows : (block + 1) * rows]
    slope_ref[...] = u * sig * (1.0 + a * (1.0 - sig))
    silu_ref[...] = silu


def slot_weight(meta, expert):
    topk = 8
    meta = meta.astype(F32)
    lane = lax.broadcasted_iota(jnp.int32, meta.shape, 1)
    weight = pltpu.roll(meta, META - topk, 1)
    return jnp.sum(jnp.where((lane < topk) & (meta == expert.astype(F32)), weight, 0.0), axis=1, keepdims=True)


def down_kernel(mine_ref, got_ref, turned_ref, keep_ref, send_ref):
    half, width = keep_ref.shape
    core = mine_ref[1]
    w = slot_weight(got_ref[:, width:], mine_ref[0])
    columns = 512
    for at in range(0, width, columns):
        scaled = (w * got_ref[:, at : at + columns].astype(F32)).astype(BF16)
        for ref, which in ((send_ref, 1 - core), (keep_ref, core)):
            begin = pl.multiple_of(which * half, half)
            ref[:, at : at + columns] = jnp.dot(
                turned_ref[pl.ds(begin, half), :], scaled, preferred_element_type=F32
            ).astype(BF16)


def fetch(pack_ref, base, wide_buf, sems, first):
    _, rows, both = wide_buf.shape
    across, per = both // TILE, pack_ref.shape[2] // TILE
    copies = []
    for i in range(rows // 16):
        for j in range(across):
            n = i * across + j
            copies.append(
                pltpu.make_async_copy(
                    pack_ref.at[:, pl.ds(base + n // per * 16, 16), pl.ds(n % per * TILE, TILE)],
                    wide_buf.at[:, pl.ds(i * 16, 16), pl.ds(j * TILE, TILE)],
                    sems.at[first + n],
                )
            )
    for copy in copies:
        copy.start()
    return copies


def multiply(both_ref, wide_buf, out_buf, out_ref, sems, backs):
    columns = 256
    devices, rows, both = wide_buf.shape
    group = columns // rows
    for n in range(devices // group):
        at = n * columns
        out_buf[:, at : at + columns] = lax.dot_general(
            both_ref[...],
            wide_buf[n * group : (n + 1) * group].reshape(columns, both),
            (((1,), (1,)), ((), ())),
            preferred_element_type=F32,
        ).astype(BF16)
        part = pl.ds(at, columns)
        backs.append(pltpu.make_async_copy(out_buf.at[:, part], out_ref.at[:, part], sems.at[n]))
        backs[-1].start()
    for copy in backs:
        copy.wait()


def mid_kernel(
    mine_ref, got_ref, hid_ref, slope_ref, silu_ref, pack_ref, out_ref,
    out_buf, both_ref, down_buf, wide_buf, in_sems, out_sems,
):
    width = got_ref.shape[1] - META
    hidden = hid_ref.shape[1]
    down_rows = down_buf.shape[1]
    down_copy = pltpu.make_async_copy(pack_ref.at[:, pl.ds(0, down_rows), :], down_buf, in_sems.at[0])
    down_copy.start()
    copies = fetch(pack_ref, down_rows, wide_buf, in_sems, 1)
    w = slot_weight(got_ref[:, width:], mine_ref[0])
    down_copy.wait()
    q = lax.dot_general(
        got_ref[:, :width],
        down_buf[...].reshape(hidden, width),
        (((1,), (1,)), ((), ())),
        preferred_element_type=F32,
    )
    route = jnp.sum(q * hid_ref[...].astype(F32), axis=1, keepdims=True)
    grad = w * q
    both_ref[:, :hidden] = (grad * slope_ref[...]).astype(BF16)
    both_ref[:, hidden:] = (grad * silu_ref[...]).astype(BF16)
    lane = lax.broadcasted_iota(jnp.int32, (got_ref.shape[0], META), 1)
    out_buf[:, width:] = jnp.where(lane == mine_ref[0], route, 0.0).astype(BF16)
    extra = pl.ds(width, META)
    last = out_sems.shape[0] - 1
    backs = [pltpu.make_async_copy(out_buf.at[:, extra], out_ref.at[:, extra], out_sems.at[last])]
    backs[0].start()
    for copy in copies:
        copy.wait()
    multiply(both_ref, wide_buf, out_buf, out_ref, out_sems, backs)


def combine_kernel(place_ref, select_ref, back_ref, own_ref, next_ref, left_ref, right_ref, before_ref, total_buf):
    tok = own_ref.shape[0]
    cut = left_ref.shape[1]
    total_buf[...] = lax.dot_general(
        select_ref[...], back_ref[...], (((0,), (0,)), ((), ())), preferred_element_type=F32
    )

    def rows(m):
        return pl.ds(pl.multiple_of(((place_ref[0] + m) % STRIDE) * tok, tok), tok)

    own_ref[...] = total_buf[rows(0), :]
    next_ref[...] = total_buf[rows(1), :]
    before_ref[...] = total_buf[rows(3), :]
    left_ref[...] = total_buf[rows(2), 0:cut].astype(BF16)
    right_ref[...] = total_buf[rows(2), cut:].astype(BF16)


def pass_kernel(base, part_ref, more_ref, out_ref):
    size = more_ref.shape[1]
    out_ref[...] = part_ref[...].astype(BF16)
    out_ref[:, base : base + size] = (part_ref[:, base : base + size] + more_ref[...].astype(F32)).astype(BF16)


def last_kernel(ids_ref, *refs):
    parts, (tok_ref, route_ref) = refs[:-2], refs[-2:]
    tok, width = tok_ref.shape
    total = parts[0][...]
    for ref in parts[1:]:
        total = total + ref[...].astype(F32)
    tok_ref[...] = total[:, :width].astype(BF16)
    route = turn(total[:, width:])
    ids = ids_ref[...]
    expert = lax.broadcasted_iota(jnp.int32, route.shape, 0)
    found = [
        jnp.sum(jnp.where(expert == ids[k : k + 1, :], route, 0.0), axis=0, keepdims=True)
        for k in range(ids.shape[0])
    ]
    route_ref[...] = jnp.concatenate(found, axis=0).astype(BF16)


def shape(dims, dtype=BF16):
    return jax.ShapeDtypeStruct(dims, dtype)


def whole(memory=pltpu.VMEM):
    return pl.BlockSpec(memory_space=memory)


def exchange(value, axes, groups):
    return lax.all_to_all(value, axes, 0, 0, axis_index_groups=groups, tiled=True)


def per_device(n_dp, n_expert, grad_out, expert_ids, route_weights, saved_pre, gate_weight, up_weight, down_weight):
    tok, width = grad_out.shape
    pre = saved_pre[0, 0]
    slots, both = pre.shape
    hidden = both // 2
    cap = slots // n_expert
    full = width + META
    n_z = n_expert // 2
    dests = slots // (cap * STRIDE)
    per = STRIDE * cap
    down_rows = down_weight.shape[1]
    axes = ("dp", "expert")

    apart = [
        [d * n_expert + (rho + STRIDE * k) * 2 + h for k in range(n_z // STRIDE)]
        for d in range(n_dp)
        for rho in range(STRIDE)
        for h in range(2)
    ]
    near = [
        [
            d * n_expert + ((STRIDE * a + (rho - 2 * (d % 2)) % STRIDE + 2 * (d % 2)) % n_z) * 2 + h
            for rho in range(STRIDE)
            for h in range(2)
        ]
        for d in range(n_dp)
        for a in range(n_z // STRIDE)
    ]
    core, me = lax.axis_index("dp") % 2, lax.axis_index("expert")
    shift = 2 * core
    quad = ((me // 2 - shift + n_z) % n_z) // STRIDE
    rho = jnp.arange(dests, dtype=jnp.int32) // 2
    members = ((STRIDE * quad + (rho - shift + STRIDE) % STRIDE + shift) % n_z) * 2 + jnp.arange(
        dests, dtype=jnp.int32
    ) % 2
    mine = jnp.stack([me, core]).astype(jnp.int32)

    wide = gate_weight.shape[1]
    part = wide * both // width
    rows, pack = pl.pallas_call(
        prep_kernel,
        out_shape=(shape((tok, full)), shape((down_rows + part, width))),
        in_specs=[whole(pltpu.HBM)] * 6,
        out_specs=(whole(),) * 2,
        scratch_shapes=[
            pltpu.VMEM((expert_ids.shape[1], tok), jnp.int32),
            pltpu.VMEM((expert_ids.shape[1], tok), BF16),
            pltpu.VMEM((wide, hidden), BF16),
            pltpu.VMEM((wide, hidden), BF16),
            pltpu.SemaphoreType.DMA((6,)),
        ],
        compiler_params=params(60),
        name="prep",
    )(grad_out, expert_ids.T, route_weights.T, gate_weight[0], up_weight[0], down_weight[0])
    packs = lax.all_gather(pack, "dp", axis=0, tiled=False)
    blocks = lax.all_gather(rows, axes, axis=0, tiled=True, axis_index_groups=apart)
    send, select = pl.pallas_call(
        functools.partial(select_kernel, cap),
        out_shape=(shape((dests, per, full)), shape((slots, STRIDE * tok))),
        in_specs=[whole(pltpu.SMEM), whole()],
        out_specs=(whole(), whole()),
        compiler_params=params(16),
        name="select",
    )(members, blocks)
    got = exchange(send, axes, near).reshape(slots, full)
    hid, turned, slope, silu = pl.pallas_call(
        functools.partial(act_kernel, cap, down_rows),
        out_shape=(
            shape((slots, hidden)),
            shape((hidden, slots)),
            shape((slots, hidden), F32),
            shape((slots, hidden), F32),
        ),
        in_specs=[whole()],
        out_specs=(whole(),) * 4,
        compiler_params=params(24),
        cost_estimate=pl.CostEstimate(flops=slots * slots * both * 2, bytes_accessed=8 * slots * both, transcendentals=0),
        name="act",
    )(pre)
    keep, give = pl.pallas_call(
        down_kernel,
        out_shape=(shape((hidden // 2, width)), shape((hidden // 2, width))),
        in_specs=[whole(pltpu.SMEM), whole(), whole()],
        out_specs=(whole(), whole()),
        compiler_params=params(20),
        cost_estimate=pl.CostEstimate(flops=2 * slots * hidden * width, bytes_accessed=2 * (slots + hidden) * width, transcendentals=0),
        name="down",
    )(mine, got, turned)
    taken = lax.ppermute(give, "dp", [(d, d ^ 1) for d in range(n_dp)])
    chip_part = (keep.astype(F32) + taken.astype(F32)).astype(BF16)
    got, chip_part = lax.optimization_barrier((got, chip_part))
    down_grad = lax.psum_scatter(
        chip_part,
        "dp",
        scatter_dimension=0,
        tiled=True,
        axis_index_groups=[list(range(c, n_dp, 2)) for c in range(2)],
    )
    columns = 256
    pieces = wide // 16 * (both // TILE)
    back = pl.pallas_call(
        mid_kernel,
        out_shape=shape((slots, full)),
        in_specs=[whole(pltpu.SMEM)] + [whole()] * 4 + [whole(pltpu.HBM)],
        out_specs=whole(pltpu.HBM),
        scratch_shapes=[
            pltpu.VMEM((slots, full), BF16),
            pltpu.VMEM((slots, both), BF16),
            pltpu.VMEM((n_dp, down_rows, width), BF16),
            pltpu.VMEM((n_dp, wide, both), BF16),
            pltpu.SemaphoreType.DMA((pieces + 1,)),
            pltpu.SemaphoreType.DMA((width // columns + 1,)),
        ],
        compiler_params=params(54),
        cost_estimate=pl.CostEstimate(flops=6 * slots * hidden * width, bytes_accessed=6 * hidden * width, transcendentals=0),
        name="mid",
    )(mine, got, hid, slope, silu, packs)
    back = exchange(back.reshape(dests, per, full), axes, near).reshape(slots, full)
    place = (me // 2 // STRIDE).reshape(1).astype(jnp.int32)
    cut = (full // META + 1) // 2 * META
    own, after, left, right, before = pl.pallas_call(
        combine_kernel,
        out_shape=(
            shape((tok, full), F32),
            shape((tok, full), F32),
            shape((tok, cut)),
            shape((tok, full - cut)),
            shape((tok, full), F32),
        ),
        in_specs=[whole(pltpu.SMEM), whole(), whole()],
        out_specs=(whole(),) * 5,
        scratch_shapes=[pltpu.VMEM((STRIDE * tok, full), F32)],
        compiler_params=params(12),
        name="combine",
    )(place, select, back)

    def hop(value, step):
        perm = [(e, ((e // 2 + step) % n_z) * 2 + e % 2) for e in range(n_expert)]
        return lax.ppermute(value, "expert", perm)

    parts = [own]
    for name, part, piece, base, step in (("up", after, left, 0, STRIDE), ("down", before, right, cut, -STRIDE)):
        out = pl.pallas_call(
            functools.partial(pass_kernel, base),
            out_shape=shape((tok, full)),
            in_specs=[whole(), whole()],
            out_specs=whole(),
            compiler_params=params(8),
            name="pass_" + name,
        )(part, hop(piece, step))
        parts.append(hop(out, step))
    token_grad, route_grad = pl.pallas_call(
        last_kernel,
        out_shape=(shape((tok, width)), shape(expert_ids.shape[::-1])),
        in_specs=[whole()] * (1 + len(parts)),
        out_specs=(whole(), whole()),
        compiler_params=params(8),
        name="last",
    )(expert_ids.T, *parts)
    return token_grad, route_grad.T, down_grad[None]


def solution(mesh):
    return jax.shard_map(
        functools.partial(per_device, mesh.shape["dp"], mesh.shape["expert"]),
        mesh=mesh,
        in_specs=(
            P(("dp", "expert"), None),
            P(("dp", "expert"), None),
            P(("dp", "expert"), None),
            P("dp", "expert", None, None),
            P("expert", "dp", None),
            P("expert", "dp", None),
            P("expert", "dp", None),
        ),
        out_specs=(P(("dp", "expert"), None), P(("dp", "expert"), None), P("expert", "dp", None)),
        check_vma=False,
    )
```

```python
import functools

import jax
import jax.numpy as jnp
from jax import lax
from jax.experimental import pallas as pl
from jax.experimental.pallas import tpu as pltpu
from jax.sharding import PartitionSpec as P

BF16, F32 = jnp.bfloat16, jnp.float32
META = 128
TILE = 512
STRIDE = 4


def params(mib):
    return pltpu.CompilerParams(vmem_limit_bytes=mib * 1024 * 1024)


def turn(values):
    rows, columns = values.shape
    if columns < META:
        values = jnp.concatenate([values, jnp.zeros((rows, META - columns), F32)], axis=1)
    if rows < META:
        values = jnp.concatenate([values, jnp.zeros((META - rows, META), F32)], axis=0)
    return values.T[:columns, :rows] if columns < META else values.T[:, :rows]


def prep_kernel(
    rows_ref, ids_ref, weight_ref, gate_ref, up_ref, down_ref, tok_ref, pack_ref,
    ids_buf, weight_buf, gate_buf, up_buf, sems,
):
    tok, width = rows_ref.shape
    topk = ids_ref.shape[0]
    hidden = gate_ref.shape[1]
    down_rows = down_ref.shape[0]
    copies = [
        pltpu.make_async_copy(gate_ref, gate_buf, sems.at[0]),
        pltpu.make_async_copy(up_ref, up_buf, sems.at[1]),
        pltpu.make_async_copy(down_ref, pack_ref.at[pl.ds(0, down_rows), :], sems.at[2]),
        pltpu.make_async_copy(ids_ref, ids_buf, sems.at[3]),
        pltpu.make_async_copy(weight_ref, weight_buf, sems.at[4]),
        pltpu.make_async_copy(rows_ref, tok_ref.at[:, pl.ds(0, width)], sems.at[5]),
    ]
    for copy in copies:
        copy.start()
    copies[0].wait()
    copies[1].wait()
    piece = TILE // 2
    for i in range(gate_ref.shape[0] // 16):
        for p in range(2 * hidden // piece):
            n = i * (2 * hidden // TILE) + p // 2
            row = down_rows + n // (width // TILE) * 16
            lane = n % (width // TILE) * TILE + p % 2 * piece
            buf = gate_buf if p * piece < hidden else up_buf
            src = p * piece % hidden
            pack_ref[row : row + 16, lane : lane + piece] = buf[i * 16 : i * 16 + 16, src : src + piece]
    copies[3].wait()
    copies[4].wait()
    meta = jnp.concatenate([ids_buf[...].astype(F32), weight_buf[...].astype(F32)], axis=0)
    meta = jnp.concatenate([meta, jnp.zeros((META - 2 * topk, tok), F32)], axis=0)
    tok_ref[:, width:] = turn(meta).astype(BF16)
    copies[2].wait()
    copies[5].wait()


def select_kernel(cap, mine_ref, tok_ref, send_ref, select_ref):
    rows, full = tok_ref.shape
    width = full - META
    dests, per, _ = send_ref.shape
    block = rows // STRIDE
    topk = 8
    ids = tok_ref[:, width:].astype(F32).T[0:topk, :]
    member = jnp.concatenate(
        [
            jnp.max((ids == mine_ref[j].astype(F32)).astype(F32), axis=0, keepdims=True)
            for j in range(dests)
        ],
        axis=0,
    )
    before = lax.broadcasted_iota(jnp.int32, (rows, rows), 0)
    after = lax.broadcasted_iota(jnp.int32, (rows, rows), 1)
    earlier = (before < after) & (before // block == after // block)
    rank = jnp.dot(member.astype(BF16), earlier.astype(BF16), preferred_element_type=F32)
    key = jnp.where(member > 0.0, rank, -1.0)
    place = lax.broadcasted_iota(jnp.int32, (per, rows), 0)
    source = lax.broadcasted_iota(jnp.int32, (per, rows), 1) // block
    pattern = jnp.where(place // cap == source, place - source * cap, -2).astype(F32)
    for j in range(dests):
        chosen = (key[j : j + 1, :] == pattern).astype(BF16)
        select_ref[j * per : (j + 1) * per, :] = chosen
    for j in range(dests):
        send_ref[j] = jnp.dot(
            select_ref[j * per : (j + 1) * per, :], tok_ref[...], preferred_element_type=F32
        ).astype(BF16)


def act_kernel(cap, rows, pre_ref, hid_ref, turned_ref, slope_ref, silu_ref):
    slots, both = pre_ref.shape
    hidden = both // 2
    dests = slots // (cap * STRIDE)
    at = lax.broadcasted_iota(jnp.int32, (slots, slots), 0)
    src = lax.broadcasted_iota(jnp.int32, (slots, slots), 1)
    j, rest = at // (STRIDE * cap), at % (STRIDE * cap)
    k, r = rest // cap, rest % cap
    order = (src == (k * dests + j) * cap + r).astype(BF16)
    a = jnp.dot(order, pre_ref[:, :hidden], preferred_element_type=F32)
    u = jnp.dot(order, pre_ref[:, hidden:], preferred_element_type=F32)
    sig = jax.nn.sigmoid(a)
    silu = a * sig
    hid = (silu * u).astype(BF16)
    hid_ref[...] = hid
    turned = hid.astype(F32).T.astype(BF16)
    for block in range(hidden // rows):
        at = (block % 2) * (hidden // 2) + (block // 2) * rows
        turned_ref[at : at + rows, :] = turned[block * rows : (block + 1) * rows]
    slope_ref[...] = u * sig * (1.0 + a * (1.0 - sig))
    silu_ref[...] = silu


def slot_weight(meta, expert):
    topk = 8
    meta = meta.astype(F32)
    lane = lax.broadcasted_iota(jnp.int32, meta.shape, 1)
    weight = pltpu.roll(meta, META - topk, 1)
    return jnp.sum(jnp.where((lane < topk) & (meta == expert.astype(F32)), weight, 0.0), axis=1, keepdims=True)


def down_kernel(mine_ref, got_ref, turned_ref, keep_ref, send_ref):
    half, width = keep_ref.shape
    core = mine_ref[1]
    w = slot_weight(got_ref[:, width:], mine_ref[0])
    columns = 512
    for at in range(0, width, columns):
        scaled = (w * got_ref[:, at : at + columns].astype(F32)).astype(BF16)
        for ref, which in ((send_ref, 1 - core), (keep_ref, core)):
            begin = pl.multiple_of(which * half, half)
            ref[:, at : at + columns] = jnp.dot(
                turned_ref[pl.ds(begin, half), :], scaled, preferred_element_type=F32
            ).astype(BF16)


def fetch(pack_ref, begin, base, wide_buf, sems, first):
    devices, rows, both = wide_buf.shape
    across, per = both // TILE, pack_ref.shape[2] // TILE
    copies = []
    for i in range(rows // 16):
        for j in range(across):
            n = i * across + j
            copies.append(
                pltpu.make_async_copy(
                    pack_ref.at[pl.ds(begin, devices), pl.ds(base + n // per * 16, 16), pl.ds(n % per * TILE, TILE)],
                    wide_buf.at[:, pl.ds(i * 16, 16), pl.ds(j * TILE, TILE)],
                    sems.at[first + n],
                )
            )
    for copy in copies:
        copy.start()
    return copies


def multiply(both_ref, wide_buf, out_buf, out_ref, sems, backs):
    columns = 256
    devices, rows, both = wide_buf.shape
    group = columns // rows
    for n in range(devices // group):
        at = n * columns
        out_buf[:, at : at + columns] = lax.dot_general(
            both_ref[...],
            wide_buf[n * group : (n + 1) * group].reshape(columns, both),
            (((1,), (1,)), ((), ())),
            preferred_element_type=F32,
        ).astype(BF16)
        part = pl.ds(at, columns)
        backs.append(pltpu.make_async_copy(out_buf.at[:, part], out_ref.at[:, part], sems.at[n]))
        backs[-1].start()
    for copy in backs:
        copy.wait()


def first_kernel(
    mine_ref, got_ref, hid_ref, slope_ref, silu_ref, pack_ref, out_ref, both_ref,
    out_buf, down_buf, wide_buf, in_sems, out_sems,
):
    width = got_ref.shape[1] - META
    hidden = hid_ref.shape[1]
    down_rows = down_buf.shape[1]
    half = out_buf.shape[1] - META
    down_copy = pltpu.make_async_copy(pack_ref.at[:, pl.ds(0, down_rows), :], down_buf, in_sems.at[0])
    down_copy.start()
    copies = fetch(pack_ref, 0, down_rows, wide_buf, in_sems, 1)
    w = slot_weight(got_ref[:, width:], mine_ref[0])
    down_copy.wait()
    q = lax.dot_general(
        got_ref[:, :width],
        down_buf[...].reshape(hidden, width),
        (((1,), (1,)), ((), ())),
        preferred_element_type=F32,
    )
    route = jnp.sum(q * hid_ref[...].astype(F32), axis=1, keepdims=True)
    grad = w * q
    both_ref[:, :hidden] = (grad * slope_ref[...]).astype(BF16)
    both_ref[:, hidden:] = (grad * silu_ref[...]).astype(BF16)
    lane = lax.broadcasted_iota(jnp.int32, (got_ref.shape[0], META), 1)
    out_buf[:, half:] = jnp.where(lane == mine_ref[0], route, 0.0).astype(BF16)
    extra = pl.ds(half, META)
    last = out_sems.shape[0] - 1
    backs = [pltpu.make_async_copy(out_buf.at[:, extra], out_ref.at[:, extra], out_sems.at[last])]
    backs[0].start()
    for copy in copies:
        copy.wait()
    multiply(both_ref, wide_buf, out_buf, out_ref, out_sems, backs)


def second_kernel(down_rows, both_ref, pack_ref, out_ref, out_buf, wide_buf, in_sems, out_sems):
    devices = wide_buf.shape[0]
    for copy in fetch(pack_ref, pack_ref.shape[0] - devices, down_rows, wide_buf, in_sems, 0):
        copy.wait()
    multiply(both_ref, wide_buf, out_buf, out_ref, out_sems, [])


def combine_kernel(place_ref, select_ref, back_ref, *refs):
    outs, total_buf = refs[:-1], refs[-1]
    tok = outs[0].shape[0]
    total_buf[...] = lax.dot_general(
        select_ref[...], back_ref[...], (((0,), (0,)), ((), ())), preferred_element_type=F32
    )
    for m, ref in enumerate(outs):
        begin = pl.multiple_of(((place_ref[0] + m) % STRIDE) * tok, tok)
        ref[...] = total_buf[pl.ds(begin, tok), :].astype(ref.dtype)


def last_kernel(ids_ref, *refs):
    first, second, (tok_ref, route_ref) = refs[:STRIDE], refs[STRIDE : 2 * STRIDE], refs[2 * STRIDE :]
    half = tok_ref.shape[1] // 2
    sums = []
    for parts in (first, second):
        total = parts[0][...]
        for ref in parts[1:]:
            total = total + ref[...].astype(F32)
        sums.append(total)
    tok_ref[:, :half] = sums[0][:, :half].astype(BF16)
    tok_ref[:, half:] = sums[1].astype(BF16)
    route = turn(sums[0][:, half:])
    ids = ids_ref[...]
    expert = lax.broadcasted_iota(jnp.int32, route.shape, 0)
    found = [
        jnp.sum(jnp.where(expert == ids[k : k + 1, :], route, 0.0), axis=0, keepdims=True)
        for k in range(ids.shape[0])
    ]
    route_ref[...] = jnp.concatenate(found, axis=0).astype(BF16)


def shape(dims, dtype=BF16):
    return jax.ShapeDtypeStruct(dims, dtype)


def whole(memory=pltpu.VMEM):
    return pl.BlockSpec(memory_space=memory)


def exchange(value, axes, groups):
    return lax.all_to_all(value, axes, 0, 0, axis_index_groups=groups, tiled=True)


def per_device(n_dp, n_expert, grad_out, expert_ids, route_weights, saved_pre, gate_weight, up_weight, down_weight):
    tok, width = grad_out.shape
    pre = saved_pre[0, 0]
    slots, both = pre.shape
    hidden = both // 2
    cap = slots // n_expert
    full = width + META
    n_z = n_expert // 2
    dests = slots // (cap * STRIDE)
    per = STRIDE * cap
    down_rows = down_weight.shape[1]
    axes = ("dp", "expert")

    apart = [
        [d * n_expert + (rho + STRIDE * k) * 2 + h for k in range(n_z // STRIDE)]
        for d in range(n_dp)
        for rho in range(STRIDE)
        for h in range(2)
    ]
    near = [
        [
            d * n_expert + ((STRIDE * a + (rho - 2 * (d % 2)) % STRIDE + 2 * (d % 2)) % n_z) * 2 + h
            for rho in range(STRIDE)
            for h in range(2)
        ]
        for d in range(n_dp)
        for a in range(n_z // STRIDE)
    ]
    core, me = lax.axis_index("dp") % 2, lax.axis_index("expert")
    shift = 2 * core
    quad = ((me // 2 - shift + n_z) % n_z) // STRIDE
    rho = jnp.arange(dests, dtype=jnp.int32) // 2
    members = ((STRIDE * quad + (rho - shift + STRIDE) % STRIDE + shift) % n_z) * 2 + jnp.arange(
        dests, dtype=jnp.int32
    ) % 2
    mine = jnp.stack([me, core]).astype(jnp.int32)

    wide = gate_weight.shape[1]
    part = wide * both // width
    rows, pack = pl.pallas_call(
        prep_kernel,
        out_shape=(shape((tok, full)), shape((down_rows + part, width))),
        in_specs=[whole(pltpu.HBM)] * 6,
        out_specs=(whole(),) * 2,
        scratch_shapes=[
            pltpu.VMEM((expert_ids.shape[1], tok), jnp.int32),
            pltpu.VMEM((expert_ids.shape[1], tok), BF16),
            pltpu.VMEM((wide, hidden), BF16),
            pltpu.VMEM((wide, hidden), BF16),
            pltpu.SemaphoreType.DMA((6,)),
        ],
        compiler_params=params(60),
        name="prep",
    )(grad_out, expert_ids.T, route_weights.T, gate_weight[0], up_weight[0], down_weight[0])
    packs = lax.all_gather(pack, "dp", axis=0, tiled=False)
    blocks = lax.all_gather(rows, axes, axis=0, tiled=True, axis_index_groups=apart)
    send, select = pl.pallas_call(
        functools.partial(select_kernel, cap),
        out_shape=(shape((dests, per, full)), shape((slots, STRIDE * tok))),
        in_specs=[whole(pltpu.SMEM), whole()],
        out_specs=(whole(), whole()),
        compiler_params=params(16),
        name="select",
    )(members, blocks)
    got = exchange(send, axes, near).reshape(slots, full)
    hid, turned, slope, silu = pl.pallas_call(
        functools.partial(act_kernel, cap, down_rows),
        out_shape=(
            shape((slots, hidden)),
            shape((hidden, slots)),
            shape((slots, hidden), F32),
            shape((slots, hidden), F32),
        ),
        in_specs=[whole()],
        out_specs=(whole(),) * 4,
        compiler_params=params(24),
        cost_estimate=pl.CostEstimate(flops=slots * slots * both * 2, bytes_accessed=8 * slots * both, transcendentals=0),
        name="act",
    )(pre)
    columns = 256
    half = width // 2
    pieces = wide // 16 * (both // TILE)
    back, grads = pl.pallas_call(
        first_kernel,
        out_shape=(shape((slots, half + META)), shape((slots, both))),
        in_specs=[whole(pltpu.SMEM)] + [whole()] * 4 + [whole(pltpu.HBM)],
        out_specs=(whole(pltpu.HBM), whole()),
        scratch_shapes=[
            pltpu.VMEM((slots, half + META), BF16),
            pltpu.VMEM((n_dp, down_rows, width), BF16),
            pltpu.VMEM((n_dp // 2, wide, both), BF16),
            pltpu.SemaphoreType.DMA((pieces + 1,)),
            pltpu.SemaphoreType.DMA((half // columns + 1,)),
        ],
        compiler_params=params(54),
        cost_estimate=pl.CostEstimate(flops=4 * slots * hidden * width, bytes_accessed=4 * hidden * width, transcendentals=0),
        name="first",
    )(mine, got, hid, slope, silu, packs)
    ret = exchange(back.reshape(dests, per, -1), axes, near).reshape(slots, -1)
    back_b = pl.pallas_call(
        functools.partial(second_kernel, down_rows),
        out_shape=shape((slots, half)),
        in_specs=[whole(), whole(pltpu.HBM)],
        out_specs=whole(pltpu.HBM),
        scratch_shapes=[
            pltpu.VMEM((slots, half), BF16),
            pltpu.VMEM((n_dp // 2, wide, both), BF16),
            pltpu.SemaphoreType.DMA((pieces,)),
            pltpu.SemaphoreType.DMA((half // columns,)),
        ],
        compiler_params=params(54),
        cost_estimate=pl.CostEstimate(flops=2 * slots * hidden * width, bytes_accessed=2 * hidden * width, transcendentals=0),
        name="second",
    )(grads, packs)

    got, back_b = lax.optimization_barrier((got, back_b))
    keep, give = pl.pallas_call(
        down_kernel,
        out_shape=(shape((hidden // 2, width)), shape((hidden // 2, width))),
        in_specs=[whole(pltpu.SMEM), whole(), whole()],
        out_specs=(whole(), whole()),
        compiler_params=params(20),
        cost_estimate=pl.CostEstimate(flops=2 * slots * hidden * width, bytes_accessed=2 * (slots + hidden) * width, transcendentals=0),
        name="down",
    )(mine, got, turned)
    taken = lax.ppermute(give, "dp", [(d, d ^ 1) for d in range(n_dp)])
    chip_part = (keep.astype(F32) + taken.astype(F32)).astype(BF16)
    ret, _ = lax.optimization_barrier((ret, chip_part))
    down_grad = lax.psum_scatter(
        chip_part,
        "dp",
        scatter_dimension=0,
        tiled=True,
        axis_index_groups=[list(range(c, n_dp, 2)) for c in range(2)],
    )
    ret, back_b = lax.optimization_barrier((ret, back_b))
    ret_b = exchange(back_b.reshape(dests, per, -1), axes, near).reshape(slots, -1)

    place = (me // 2 // STRIDE).reshape(1).astype(jnp.int32)
    parts = []
    for name, value in (("sum_first", ret), ("sum_second", ret_b)):
        dims = (tok, value.shape[1])
        own, *sums = pl.pallas_call(
            combine_kernel,
            out_shape=(shape(dims, F32),) + (shape(dims),) * (STRIDE - 1),
            in_specs=[whole(pltpu.SMEM), whole(), whole()],
            out_specs=(whole(),) * STRIDE,
            scratch_shapes=[pltpu.VMEM((STRIDE * tok, value.shape[1]), F32)],
            compiler_params=params(12),
            name=name,
        )(place, select, value)
        parts.append(own)
        for m, one in enumerate(sums):
            perm = [(e, ((e // 2 + STRIDE * (m + 1)) % n_z) * 2 + e % 2) for e in range(n_expert)]
            parts.append(lax.ppermute(one, "expert", perm))
    token_grad, route_grad = pl.pallas_call(
        last_kernel,
        out_shape=(shape((tok, width)), shape(expert_ids.shape[::-1])),
        in_specs=[whole()] * (1 + len(parts)),
        out_specs=(whole(), whole()),
        compiler_params=params(8),
        name="last",
    )(expert_ids.T, *parts)
    return token_grad, route_grad.T, down_grad[None]


def solution(mesh):
    return jax.shard_map(
        functools.partial(per_device, mesh.shape["dp"], mesh.shape["expert"]),
        mesh=mesh,
        in_specs=(
            P(("dp", "expert"), None),
            P(("dp", "expert"), None),
            P(("dp", "expert"), None),
            P("dp", "expert", None, None),
            P("expert", "dp", None),
            P("expert", "dp", None),
            P("expert", "dp", None),
        ),
        out_specs=(P(("dp", "expert"), None), P(("dp", "expert"), None), P("expert", "dp", None)),
        check_vma=False,
    )
```

```python
import functools

import jax
import jax.numpy as jnp
from jax import lax
from jax.experimental import pallas as pl
from jax.experimental.pallas import tpu as pltpu
from jax.sharding import PartitionSpec as P

BF16, F32 = jnp.bfloat16, jnp.float32
META = 128
STRIDE = 4


def params(mib):
    return pltpu.CompilerParams(vmem_limit_bytes=mib * 1024 * 1024)


def turn(values):
    rows, columns = values.shape
    if columns < META:
        values = jnp.concatenate([values, jnp.zeros((rows, META - columns), F32)], axis=1)
    if rows < META:
        values = jnp.concatenate([values, jnp.zeros((META - rows, META), F32)], axis=0)
    return values.T[:columns, :rows] if columns < META else values.T[:, :rows]


def prep_kernel(
    rows_ref, ids_ref, weight_ref, gate_ref, up_ref, down_ref, tok_ref, pack_ref, downs_ref,
    ids_buf, weight_buf, down_buf, sems,
):
    tok, width = rows_ref.shape
    topk = ids_ref.shape[0]
    hidden = gate_ref.shape[1]
    copies = [
        pltpu.make_async_copy(gate_ref, pack_ref.at[:, pl.ds(0, hidden)], sems.at[0]),
        pltpu.make_async_copy(up_ref, pack_ref.at[:, pl.ds(hidden, hidden)], sems.at[1]),
        pltpu.make_async_copy(ids_ref, ids_buf, sems.at[2]),
        pltpu.make_async_copy(weight_ref, weight_buf, sems.at[3]),
        pltpu.make_async_copy(rows_ref, tok_ref.at[:, pl.ds(0, width)], sems.at[4]),
        pltpu.make_async_copy(down_ref, down_buf, sems.at[5]),
    ]
    for copy in copies:
        copy.start()
    copies[5].wait()
    outs = [
        pltpu.make_async_copy(down_buf, downs_ref.at[i], sems.at[6 + i]) for i in range(downs_ref.shape[0])
    ]
    for copy in outs:
        copy.start()
    copies[2].wait()
    copies[3].wait()
    meta = jnp.concatenate([ids_buf[...].astype(F32), weight_buf[...].astype(F32)], axis=0)
    meta = jnp.concatenate([meta, jnp.zeros((META - 2 * topk, tok), F32)], axis=0)
    tok_ref[:, width:] = turn(meta).astype(BF16)
    for copy in copies[:2] + copies[4:5] + outs:
        copy.wait()


def select_kernel(cap, mine_ref, tok_ref, send_ref, select_ref):
    rows, full = tok_ref.shape
    width = full - META
    dests, per, _ = send_ref.shape
    block = rows // STRIDE
    topk = 8
    ids = tok_ref[:, width:].astype(F32).T[0:topk, :]
    member = jnp.concatenate(
        [
            jnp.max((ids == mine_ref[j].astype(F32)).astype(F32), axis=0, keepdims=True)
            for j in range(dests)
        ],
        axis=0,
    )
    before = lax.broadcasted_iota(jnp.int32, (rows, rows), 0)
    after = lax.broadcasted_iota(jnp.int32, (rows, rows), 1)
    earlier = (before < after) & (before // block == after // block)
    rank = jnp.dot(member.astype(BF16), earlier.astype(BF16), preferred_element_type=F32)
    key = jnp.where(member > 0.0, rank, -1.0)
    place = lax.broadcasted_iota(jnp.int32, (per, rows), 0)
    source = lax.broadcasted_iota(jnp.int32, (per, rows), 1) // block
    pattern = jnp.where(place // cap == source, place - source * cap, -2).astype(F32)
    for j in range(dests):
        chosen = (key[j : j + 1, :] == pattern).astype(BF16)
        select_ref[j * per : (j + 1) * per, :] = chosen
    sent = jnp.dot(select_ref[...], tok_ref[...], preferred_element_type=F32).astype(BF16)
    send_ref[...] = sent.reshape(send_ref.shape)


def act_kernel(cap, rows, pre_ref, hid_ref, turned_ref, slope_ref, silu_ref):
    slots, both = pre_ref.shape
    hidden = both // 2
    dests = slots // (cap * STRIDE)
    at = lax.broadcasted_iota(jnp.int32, (slots, slots), 0)
    src = lax.broadcasted_iota(jnp.int32, (slots, slots), 1)
    j, rest = at // (STRIDE * cap), at % (STRIDE * cap)
    k, r = rest // cap, rest % cap
    order = (src == (k * dests + j) * cap + r).astype(BF16)
    a = jnp.dot(order, pre_ref[:, :hidden], preferred_element_type=F32)
    u = jnp.dot(order, pre_ref[:, hidden:], preferred_element_type=F32)
    sig = jax.nn.sigmoid(a)
    silu = a * sig
    hid = (silu * u).astype(BF16)
    hid_ref[...] = hid
    turned = hid.astype(F32).T.astype(BF16)
    for block in range(hidden // rows):
        at = (block % 2) * (hidden // 2) + (block // 2) * rows
        turned_ref[at : at + rows, :] = turned[block * rows : (block + 1) * rows]
    slope_ref[...] = u * sig * (1.0 + a * (1.0 - sig))
    silu_ref[...] = silu


def slot_weight(meta, expert):
    topk = 8
    meta = meta.astype(F32)
    lane = lax.broadcasted_iota(jnp.int32, meta.shape, 1)
    weight = pltpu.roll(meta, META - topk, 1)
    return jnp.sum(jnp.where((lane < topk) & (meta == expert.astype(F32)), weight, 0.0), axis=1, keepdims=True)


def down_kernel(mine_ref, got_ref, turned_ref, keep_ref, send_ref):
    half, width = keep_ref.shape
    core = mine_ref[1]
    w = slot_weight(got_ref[:, width:], mine_ref[0])
    columns = 512
    for at in range(0, width, columns):
        scaled = (w * got_ref[:, at : at + columns].astype(F32)).astype(BF16)
        for ref, which in ((send_ref, 1 - core), (keep_ref, core)):
            begin = pl.multiple_of(which * half, half)
            ref[:, at : at + columns] = jnp.dot(
                turned_ref[pl.ds(begin, half), :], scaled, preferred_element_type=F32
            ).astype(BF16)


def mid_kernel(
    mine_ref, got_ref, hid_ref, slope_ref, silu_ref, own_ref, other_ref, pack_ref, out_ref,
    out_buf, both_buf, down_buf, wide_buf, in_sems, out_sems,
):
    width = got_ref.shape[1] - META
    hidden = hid_ref.shape[1]
    devices, wide, both = wide_buf.shape
    core = mine_ref[1]
    copies = [
        pltpu.make_async_copy(own_ref, down_buf.at[:, core], in_sems.at[0]),
        pltpu.make_async_copy(other_ref, down_buf.at[:, 1 - core], in_sems.at[1]),
        pltpu.make_async_copy(pack_ref, wide_buf, in_sems.at[2]),
    ]
    for copy in copies:
        copy.start()
    w = slot_weight(got_ref[:, width:], mine_ref[0])
    copies[0].wait()
    copies[1].wait()
    q = lax.dot_general(
        got_ref[:, :width],
        down_buf[...].reshape(hidden, width),
        (((1,), (1,)), ((), ())),
        preferred_element_type=F32,
    )
    route = jnp.sum(q * hid_ref[...].astype(F32), axis=1, keepdims=True)
    grad = w * q
    both_buf[:, :hidden] = (grad * slope_ref[...]).astype(BF16)
    both_buf[:, hidden:] = (grad * silu_ref[...]).astype(BF16)
    lane = lax.broadcasted_iota(jnp.int32, (got_ref.shape[0], META), 1)
    out_buf[:, width:] = jnp.where(lane == mine_ref[0], route, 0.0).astype(BF16)
    copies[2].wait()
    backs = []
    steps = out_sems.shape[0]
    group = devices // steps
    for n in range(steps):
        at, size = n * group * wide, group * wide
        out_buf[:, at : at + size] = lax.dot_general(
            both_buf[...],
            wide_buf[n * group : (n + 1) * group].reshape(size, both),
            (((1,), (1,)), ((), ())),
            preferred_element_type=F32,
        ).astype(BF16)
        part = pl.ds(at, size + META if n == steps - 1 else size)
        backs.append(pltpu.make_async_copy(out_buf.at[:, part], out_ref.at[:, part], out_sems.at[n]))
        backs[-1].start()
    for copy in backs:
        copy.wait()


def combine_kernel(place_ref, select_ref, back_ref, own_ref, next_ref, left_ref, right_ref, before_ref, total_buf):
    tok = own_ref.shape[0]
    cut = left_ref.shape[1]
    total_buf[...] = lax.dot_general(
        select_ref[...], back_ref[...], (((0,), (0,)), ((), ())), preferred_element_type=F32
    )

    def rows(m):
        return pl.ds(pl.multiple_of(((place_ref[0] + m) % STRIDE) * tok, tok), tok)

    own_ref[...] = total_buf[rows(0), :]
    next_ref[...] = total_buf[rows(1), :]
    before_ref[...] = total_buf[rows(3), :]
    left_ref[...] = total_buf[rows(2), 0:cut].astype(BF16)
    right_ref[...] = total_buf[rows(2), cut:].astype(BF16)


def pass_kernel(base, part_ref, more_ref, out_ref):
    size = more_ref.shape[1]
    out_ref[...] = part_ref[...].astype(BF16)
    out_ref[:, base : base + size] = (part_ref[:, base : base + size] + more_ref[...].astype(F32)).astype(BF16)


def last_kernel(ids_ref, *refs):
    parts, (tok_ref, route_ref) = refs[:-2], refs[-2:]
    tok, width = tok_ref.shape
    total = parts[0][...]
    for ref in parts[1:]:
        total = total + ref[...].astype(F32)
    tok_ref[...] = total[:, :width].astype(BF16)
    route = turn(total[:, width:])
    ids = ids_ref[...]
    expert = lax.broadcasted_iota(jnp.int32, route.shape, 0)
    found = [
        jnp.sum(jnp.where(expert == ids[k : k + 1, :], route, 0.0), axis=0, keepdims=True)
        for k in range(ids.shape[0])
    ]
    route_ref[...] = jnp.concatenate(found, axis=0).astype(BF16)


def shape(dims, dtype=BF16):
    return jax.ShapeDtypeStruct(dims, dtype)


def whole(memory=pltpu.VMEM):
    return pl.BlockSpec(memory_space=memory)


def exchange(value, axes, groups):
    return lax.all_to_all(value, axes, 0, 0, axis_index_groups=groups, tiled=True)


def per_device(n_dp, n_expert, grad_out, expert_ids, route_weights, saved_pre, gate_weight, up_weight, down_weight):
    tok, width = grad_out.shape
    pre = saved_pre[0, 0]
    slots, both = pre.shape
    hidden = both // 2
    cap = slots // n_expert
    full = width + META
    n_z = n_expert // 2
    dests = slots // (cap * STRIDE)
    per = STRIDE * cap
    down_rows = down_weight.shape[1]
    axes = ("dp", "expert")

    apart = [
        [d * n_expert + (rho + STRIDE * k) * 2 + h for k in range(n_z // STRIDE)]
        for d in range(n_dp)
        for rho in range(STRIDE)
        for h in range(2)
    ]
    near = [
        [
            d * n_expert + ((STRIDE * a + (rho - 2 * (d % 2)) % STRIDE + 2 * (d % 2)) % n_z) * 2 + h
            for rho in range(STRIDE)
            for h in range(2)
        ]
        for d in range(n_dp)
        for a in range(n_z // STRIDE)
    ]
    core, me = lax.axis_index("dp") % 2, lax.axis_index("expert")
    shift = 2 * core
    quad = ((me // 2 - shift + n_z) % n_z) // STRIDE
    rho = jnp.arange(dests, dtype=jnp.int32) // 2
    members = ((STRIDE * quad + (rho - shift + STRIDE) % STRIDE + shift) % n_z) * 2 + jnp.arange(
        dests, dtype=jnp.int32
    ) % 2
    mine = jnp.stack([me, core]).astype(jnp.int32)

    wide = gate_weight.shape[1]
    chips = n_dp // 2
    rows, pack, downs = pl.pallas_call(
        prep_kernel,
        out_shape=(shape((tok, full)), shape((wide, both)), shape((chips, down_rows, width))),
        in_specs=[whole(pltpu.HBM)] * 6,
        out_specs=(whole(), whole(), whole(pltpu.HBM)),
        scratch_shapes=[
            pltpu.VMEM((expert_ids.shape[1], tok), jnp.int32),
            pltpu.VMEM((expert_ids.shape[1], tok), BF16),
            pltpu.VMEM((down_rows, width), BF16),
            pltpu.SemaphoreType.DMA((6 + chips,)),
        ],
        compiler_params=params(60),
        name="prep",
    )(grad_out, expert_ids.T, route_weights.T, gate_weight[0], up_weight[0], down_weight[0])
    packs = lax.all_gather(pack, "dp", axis=0, tiled=False)
    same_core = [
        [d * n_expert + e for d in range(c, n_dp, 2)] for c in range(2) for e in range(n_expert)
    ]
    swap = [(d, d ^ 1) for d in range(n_dp)]
    own_down = exchange(downs, axes, same_core)
    blocks = lax.all_gather(rows, axes, axis=0, tiled=True, axis_index_groups=apart)
    send, select = pl.pallas_call(
        functools.partial(select_kernel, cap),
        out_shape=(shape((dests, per, full)), shape((slots, STRIDE * tok))),
        in_specs=[whole(pltpu.SMEM), whole()],
        out_specs=(whole(), whole()),
        compiler_params=params(16),
        name="select",
    )(members, blocks)
    own_down, send = lax.optimization_barrier((own_down, send))
    other_down = lax.ppermute(own_down, "dp", swap)
    got = exchange(send, axes, near).reshape(slots, full)
    hid, turned, slope, silu = pl.pallas_call(
        functools.partial(act_kernel, cap, down_rows),
        out_shape=(
            shape((slots, hidden)),
            shape((hidden, slots)),
            shape((slots, hidden), F32),
            shape((slots, hidden), F32),
        ),
        in_specs=[whole()],
        out_specs=(whole(),) * 4,
        compiler_params=params(24),
        cost_estimate=pl.CostEstimate(flops=slots * slots * both * 2, bytes_accessed=8 * slots * both, transcendentals=0),
        name="act",
    )(pre)
    back = pl.pallas_call(
        mid_kernel,
        out_shape=shape((slots, full)),
        in_specs=[whole(pltpu.SMEM)] + [whole()] * 4 + [whole(pltpu.HBM)] * 3,
        out_specs=whole(pltpu.HBM),
        scratch_shapes=[
            pltpu.VMEM((slots, full), BF16),
            pltpu.VMEM((slots, both), BF16),
            pltpu.VMEM((chips, 2, down_rows, width), BF16),
            pltpu.VMEM((n_dp, wide, both), BF16),
            pltpu.SemaphoreType.DMA((3,)),
            pltpu.SemaphoreType.DMA((4,)),
        ],
        compiler_params=params(54),
        cost_estimate=pl.CostEstimate(flops=6 * slots * hidden * width, bytes_accessed=6 * hidden * width, transcendentals=0),
        name="mid",
    )(mine, got, hid, slope, silu, own_down, other_down, packs)
    got, _ = lax.optimization_barrier((got, back))
    keep, give = pl.pallas_call(
        down_kernel,
        out_shape=(shape((hidden // 2, width)), shape((hidden // 2, width))),
        in_specs=[whole(pltpu.SMEM), whole(), whole()],
        out_specs=(whole(), whole()),
        compiler_params=params(20),
        cost_estimate=pl.CostEstimate(flops=2 * slots * hidden * width, bytes_accessed=2 * (slots + hidden) * width, transcendentals=0),
        name="down",
    )(mine, got, turned)
    taken = lax.ppermute(give, "dp", swap)
    chip_part = (keep.astype(F32) + taken.astype(F32)).astype(BF16)
    down_grad = lax.psum_scatter(
        chip_part,
        "dp",
        scatter_dimension=0,
        tiled=True,
        axis_index_groups=[list(range(c, n_dp, 2)) for c in range(2)],
    )
    back = exchange(back.reshape(dests, per, full), axes, near).reshape(slots, full)
    back, _ = lax.optimization_barrier((back, chip_part))
    place = (me // 2 // STRIDE).reshape(1).astype(jnp.int32)
    cut = (full // META + 1) // 2 * META
    own, after, left, right, before = pl.pallas_call(
        combine_kernel,
        out_shape=(
            shape((tok, full), F32),
            shape((tok, full), F32),
            shape((tok, cut)),
            shape((tok, full - cut)),
            shape((tok, full), F32),
        ),
        in_specs=[whole(pltpu.SMEM), whole(), whole()],
        out_specs=(whole(),) * 5,
        scratch_shapes=[pltpu.VMEM((STRIDE * tok, full), F32)],
        compiler_params=params(12),
        name="combine",
    )(place, select, back)

    def hop(value, step):
        perm = [(e, ((e // 2 + step) % n_z) * 2 + e % 2) for e in range(n_expert)]
        return lax.ppermute(value, "expert", perm)

    parts = [own]
    for name, part, piece, base, step in (("up", after, left, 0, STRIDE), ("down", before, right, cut, -STRIDE)):
        out = pl.pallas_call(
            functools.partial(pass_kernel, base),
            out_shape=shape((tok, full)),
            in_specs=[whole(), whole()],
            out_specs=whole(),
            compiler_params=params(8),
            name="pass_" + name,
        )(part, hop(piece, step))
        parts.append(hop(out, step))
    token_grad, route_grad = pl.pallas_call(
        last_kernel,
        out_shape=(shape((tok, width)), shape(expert_ids.shape[::-1])),
        in_specs=[whole()] * (1 + len(parts)),
        out_specs=(whole(), whole()),
        compiler_params=params(8),
        name="last",
    )(expert_ids.T, *parts)
    return token_grad, route_grad.T, down_grad[None]


def solution(mesh):
    return jax.shard_map(
        functools.partial(per_device, mesh.shape["dp"], mesh.shape["expert"]),
        mesh=mesh,
        in_specs=(
            P(("dp", "expert"), None),
            P(("dp", "expert"), None),
            P(("dp", "expert"), None),
            P("dp", "expert", None, None),
            P("expert", "dp", None),
            P("expert", "dp", None),
            P("expert", "dp", None),
        ),
        out_specs=(P(("dp", "expert"), None), P(("dp", "expert"), None), P("expert", "dp", None)),
        check_vma=False,
    )
```

```python
import functools

import jax
import jax.numpy as jnp
from jax import lax
from jax.experimental import pallas as pl
from jax.experimental.pallas import tpu as pltpu
from jax.sharding import PartitionSpec as P

BF16, F32 = jnp.bfloat16, jnp.float32
META = 128
STRIDE = 4


def params(mib):
    return pltpu.CompilerParams(vmem_limit_bytes=mib * 1024 * 1024)


def turn(values):
    rows, columns = values.shape
    if columns < META:
        values = jnp.concatenate([values, jnp.zeros((rows, META - columns), F32)], axis=1)
    if rows < META:
        values = jnp.concatenate([values, jnp.zeros((META - rows, META), F32)], axis=0)
    return values.T[:columns, :rows] if columns < META else values.T[:, :rows]


def prep_kernel(
    rows_ref, ids_ref, weight_ref, gate_ref, up_ref, down_ref, tok_ref, pack_ref, downs_ref,
    tok_buf, pack_buf, down_buf, ids_buf, weight_buf, in_sems, out_sems,
):
    tok, width = rows_ref.shape
    topk = ids_ref.shape[0]
    hidden = gate_ref.shape[1]
    copies = [
        pltpu.make_async_copy(ids_ref, ids_buf, in_sems.at[0]),
        pltpu.make_async_copy(weight_ref, weight_buf, in_sems.at[1]),
        pltpu.make_async_copy(down_ref, down_buf, in_sems.at[2]),
        pltpu.make_async_copy(rows_ref, tok_buf.at[:, pl.ds(0, width)], in_sems.at[3]),
        pltpu.make_async_copy(gate_ref, pack_buf.at[:, pl.ds(0, hidden)], in_sems.at[4]),
        pltpu.make_async_copy(up_ref, pack_buf.at[:, pl.ds(hidden, hidden)], in_sems.at[5]),
    ]
    for copy in copies:
        copy.start()
    copies[0].wait()
    copies[1].wait()
    meta = jnp.concatenate([ids_buf[...].astype(F32), weight_buf[...].astype(F32)], axis=0)
    meta = jnp.concatenate([meta, jnp.zeros((META - 2 * topk, tok), F32)], axis=0)
    tok_buf[:, width:] = turn(meta).astype(BF16)
    copies[2].wait()
    outs = [
        pltpu.make_async_copy(down_buf, downs_ref.at[i], out_sems.at[2 + i]) for i in range(downs_ref.shape[0])
    ]
    for copy in outs:
        copy.start()
    copies[3].wait()
    outs.append(pltpu.make_async_copy(tok_buf, tok_ref, out_sems.at[0]))
    outs[-1].start()
    copies[4].wait()
    copies[5].wait()
    outs.append(pltpu.make_async_copy(pack_buf, pack_ref, out_sems.at[1]))
    outs[-1].start()
    for copy in outs:
        copy.wait()


def select_kernel(cap, mine_ref, tok_ref, send_ref, select_ref):
    rows, full = tok_ref.shape
    width = full - META
    dests, per, _ = send_ref.shape
    block = rows // STRIDE
    topk = 8
    ids = tok_ref[:, width:].astype(F32).T[0:topk, :]
    member = jnp.concatenate(
        [
            jnp.max((ids == mine_ref[j].astype(F32)).astype(F32), axis=0, keepdims=True)
            for j in range(dests)
        ],
        axis=0,
    )
    before = lax.broadcasted_iota(jnp.int32, (rows, rows), 0)
    after = lax.broadcasted_iota(jnp.int32, (rows, rows), 1)
    earlier = (before < after) & (before // block == after // block)
    rank = jnp.dot(member.astype(BF16), earlier.astype(BF16), preferred_element_type=F32)
    key = jnp.where(member > 0.0, rank, -1.0)
    place = lax.broadcasted_iota(jnp.int32, (per, rows), 0)
    source = lax.broadcasted_iota(jnp.int32, (per, rows), 1) // block
    pattern = jnp.where(place // cap == source, place - source * cap, -2).astype(F32)
    for j in range(dests):
        chosen = (key[j : j + 1, :] == pattern).astype(BF16)
        select_ref[j * per : (j + 1) * per, :] = chosen
    sent = jnp.dot(select_ref[...], tok_ref[...], preferred_element_type=F32).astype(BF16)
    send_ref[...] = sent.reshape(send_ref.shape)


def act_kernel(cap, rows, pre_ref, hid_ref, turned_ref, slope_ref, silu_ref):
    slots, both = pre_ref.shape
    hidden = both // 2
    dests = slots // (cap * STRIDE)
    at = lax.broadcasted_iota(jnp.int32, (slots, slots), 0)
    src = lax.broadcasted_iota(jnp.int32, (slots, slots), 1)
    j, rest = at // (STRIDE * cap), at % (STRIDE * cap)
    k, r = rest // cap, rest % cap
    order = (src == (k * dests + j) * cap + r).astype(BF16)
    a = jnp.dot(order, pre_ref[:, :hidden], preferred_element_type=F32)
    u = jnp.dot(order, pre_ref[:, hidden:], preferred_element_type=F32)
    sig = jax.nn.sigmoid(a)
    silu = a * sig
    hid = (silu * u).astype(BF16)
    hid_ref[...] = hid
    turned = hid.astype(F32).T.astype(BF16)
    for block in range(hidden // rows):
        at = (block % 2) * (hidden // 2) + (block // 2) * rows
        turned_ref[at : at + rows, :] = turned[block * rows : (block + 1) * rows]
    slope_ref[...] = u * sig * (1.0 + a * (1.0 - sig))
    silu_ref[...] = silu


def slot_weight(meta, expert):
    topk = 8
    meta = meta.astype(F32)
    lane = lax.broadcasted_iota(jnp.int32, meta.shape, 1)
    weight = pltpu.roll(meta, META - topk, 1)
    return jnp.sum(jnp.where((lane < topk) & (meta == expert.astype(F32)), weight, 0.0), axis=1, keepdims=True)


def down_kernel(mine_ref, scaled_ref, turned_ref, keep_ref, send_ref):
    half, width = keep_ref.shape
    core = mine_ref[1]
    columns = 512
    for at in range(0, width, columns):
        for ref, which in ((send_ref, 1 - core), (keep_ref, core)):
            begin = pl.multiple_of(which * half, half)
            ref[:, at : at + columns] = jnp.dot(
                turned_ref[pl.ds(begin, half), :], scaled_ref[:, at : at + columns], preferred_element_type=F32
            ).astype(BF16)


def mid_kernel(
    mine_ref, got_ref, own_ref, other_ref, hid_ref, slope_ref, silu_ref, pack_ref, out_ref, scaled_ref,
    out_buf, both_buf, scaled_buf, down_buf, hid_buf, slope_buf, silu_buf, wide_buf, in_sems, out_sems,
):
    width = got_ref.shape[1] - META
    hidden = hid_ref.shape[1]
    devices, wide, both = wide_buf.shape
    core = mine_ref[1]
    places = (
        (own_ref, down_buf.at[:, core]),
        (other_ref, down_buf.at[:, 1 - core]),
        (hid_ref, hid_buf),
        (slope_ref, slope_buf),
        (silu_ref, silu_buf),
        (pack_ref, wide_buf),
    )
    copies = [pltpu.make_async_copy(src, dst, in_sems.at[n]) for n, (src, dst) in enumerate(places)]
    for copy in copies:
        copy.start()
    w = slot_weight(got_ref[:, width:], mine_ref[0])
    scaled_buf[...] = (w * got_ref[:, :width].astype(F32)).astype(BF16)
    steps = out_sems.shape[0] - 1
    backs = [pltpu.make_async_copy(scaled_buf, scaled_ref, out_sems.at[steps])]
    backs[0].start()
    copies[0].wait()
    copies[1].wait()
    q = lax.dot_general(
        got_ref[:, :width],
        down_buf[...].reshape(hidden, width),
        (((1,), (1,)), ((), ())),
        preferred_element_type=F32,
    )
    for copy in copies[2:5]:
        copy.wait()
    route = jnp.sum(q * hid_buf[...].astype(F32), axis=1, keepdims=True)
    grad = w * q
    both_buf[:, :hidden] = (grad * slope_buf[...]).astype(BF16)
    both_buf[:, hidden:] = (grad * silu_buf[...]).astype(BF16)
    lane = lax.broadcasted_iota(jnp.int32, (got_ref.shape[0], META), 1)
    out_buf[:, width:] = jnp.where(lane == mine_ref[0], route, 0.0).astype(BF16)
    copies[5].wait()
    group = devices // steps
    for n in range(steps):
        at, size = n * group * wide, group * wide
        out_buf[:, at : at + size] = lax.dot_general(
            both_buf[...],
            wide_buf[n * group : (n + 1) * group].reshape(size, both),
            (((1,), (1,)), ((), ())),
            preferred_element_type=F32,
        ).astype(BF16)
        part = pl.ds(at, size + META if n == steps - 1 else size)
        backs.append(pltpu.make_async_copy(out_buf.at[:, part], out_ref.at[:, part], out_sems.at[n]))
        backs[-1].start()
    for copy in backs:
        copy.wait()


def combine_kernel(place_ref, select_ref, back_ref, own_ref, next_ref, left_ref, right_ref, before_ref, total_buf):
    tok = own_ref.shape[0]
    cut = left_ref.shape[1]
    total_buf[...] = lax.dot_general(
        select_ref[...], back_ref[...], (((0,), (0,)), ((), ())), preferred_element_type=F32
    )

    def rows(m):
        return pl.ds(pl.multiple_of(((place_ref[0] + m) % STRIDE) * tok, tok), tok)

    own_ref[...] = total_buf[rows(0), :]
    next_ref[...] = total_buf[rows(1), :]
    before_ref[...] = total_buf[rows(3), :]
    left_ref[...] = total_buf[rows(2), 0:cut].astype(BF16)
    right_ref[...] = total_buf[rows(2), cut:].astype(BF16)


def pass_kernel(base, part_ref, more_ref, out_ref):
    size = more_ref.shape[1]
    out_ref[...] = part_ref[...].astype(BF16)
    out_ref[:, base : base + size] = (part_ref[:, base : base + size] + more_ref[...].astype(F32)).astype(BF16)


def last_kernel(ids_ref, *refs):
    parts, (tok_ref, route_ref) = refs[:-2], refs[-2:]
    tok, width = tok_ref.shape
    total = parts[0][...]
    for ref in parts[1:]:
        total = total + ref[...].astype(F32)
    tok_ref[...] = total[:, :width].astype(BF16)
    route = turn(total[:, width:])
    ids = ids_ref[...]
    expert = lax.broadcasted_iota(jnp.int32, route.shape, 0)
    found = [
        jnp.sum(jnp.where(expert == ids[k : k + 1, :], route, 0.0), axis=0, keepdims=True)
        for k in range(ids.shape[0])
    ]
    route_ref[...] = jnp.concatenate(found, axis=0).astype(BF16)


def shape(dims, dtype=BF16):
    return jax.ShapeDtypeStruct(dims, dtype)


def whole(memory=pltpu.VMEM):
    return pl.BlockSpec(memory_space=memory)


def exchange(value, axes, groups):
    return lax.all_to_all(value, axes, 0, 0, axis_index_groups=groups, tiled=True)


def per_device(n_dp, n_expert, grad_out, expert_ids, route_weights, saved_pre, gate_weight, up_weight, down_weight):
    tok, width = grad_out.shape
    pre = saved_pre[0, 0]
    slots, both = pre.shape
    hidden = both // 2
    cap = slots // n_expert
    full = width + META
    n_z = n_expert // 2
    dests = slots // (cap * STRIDE)
    per = STRIDE * cap
    down_rows = down_weight.shape[1]
    axes = ("dp", "expert")

    apart = [
        [d * n_expert + (rho + STRIDE * k) * 2 + h for k in range(n_z // STRIDE)]
        for d in range(n_dp)
        for rho in range(STRIDE)
        for h in range(2)
    ]
    near = [
        [
            d * n_expert + ((STRIDE * a + (rho - 2 * (d % 2)) % STRIDE + 2 * (d % 2)) % n_z) * 2 + h
            for rho in range(STRIDE)
            for h in range(2)
        ]
        for d in range(n_dp)
        for a in range(n_z // STRIDE)
    ]
    core, me = lax.axis_index("dp") % 2, lax.axis_index("expert")
    shift = 2 * core
    quad = ((me // 2 - shift + n_z) % n_z) // STRIDE
    rho = jnp.arange(dests, dtype=jnp.int32) // 2
    members = ((STRIDE * quad + (rho - shift + STRIDE) % STRIDE + shift) % n_z) * 2 + jnp.arange(
        dests, dtype=jnp.int32
    ) % 2
    mine = jnp.stack([me, core]).astype(jnp.int32)

    wide = gate_weight.shape[1]
    chips = n_dp // 2
    rows, pack, downs = pl.pallas_call(
        prep_kernel,
        out_shape=(shape((tok, full)), shape((wide, both)), shape((chips, down_rows, width))),
        in_specs=[whole(pltpu.HBM)] * 6,
        out_specs=(whole(pltpu.HBM),) * 3,
        scratch_shapes=[
            pltpu.VMEM((tok, full), BF16),
            pltpu.VMEM((wide, both), BF16),
            pltpu.VMEM((down_rows, width), BF16),
            pltpu.VMEM((expert_ids.shape[1], tok), jnp.int32),
            pltpu.VMEM((expert_ids.shape[1], tok), BF16),
            pltpu.SemaphoreType.DMA((6,)),
            pltpu.SemaphoreType.DMA((2 + chips,)),
        ],
        compiler_params=params(60),
        name="prep",
    )(grad_out, expert_ids.T, route_weights.T, gate_weight[0], up_weight[0], down_weight[0])
    packs = lax.all_gather(pack, "dp", axis=0, tiled=False)
    same_core = [
        [d * n_expert + e for d in range(c, n_dp, 2)] for c in range(2) for e in range(n_expert)
    ]
    swap = [(d, d ^ 1) for d in range(n_dp)]
    own_down = exchange(downs, axes, same_core)
    blocks = lax.all_gather(rows, axes, axis=0, tiled=True, axis_index_groups=apart)
    send, select = pl.pallas_call(
        functools.partial(select_kernel, cap),
        out_shape=(shape((dests, per, full)), shape((slots, STRIDE * tok))),
        in_specs=[whole(pltpu.SMEM), whole()],
        out_specs=(whole(), whole()),
        compiler_params=params(16),
        name="select",
    )(members, blocks)
    own_down, send = lax.optimization_barrier((own_down, send))
    other_down = lax.ppermute(own_down, "dp", swap)
    got = exchange(send, axes, near).reshape(slots, full)
    hid, turned, slope, silu = pl.pallas_call(
        functools.partial(act_kernel, cap, down_rows),
        out_shape=(
            shape((slots, hidden)),
            shape((hidden, slots)),
            shape((slots, hidden), F32),
            shape((slots, hidden), F32),
        ),
        in_specs=[whole()],
        out_specs=(whole(),) * 4,
        compiler_params=params(24),
        cost_estimate=pl.CostEstimate(flops=slots * slots * both * 2, bytes_accessed=8 * slots * both, transcendentals=0),
        name="act",
    )(pre)
    back, scaled = pl.pallas_call(
        mid_kernel,
        out_shape=(shape((slots, full)), shape((slots, width))),
        in_specs=[whole(pltpu.SMEM), whole()] + [whole(pltpu.HBM)] * 6,
        out_specs=(whole(pltpu.HBM),) * 2,
        scratch_shapes=[
            pltpu.VMEM((slots, full), BF16),
            pltpu.VMEM((slots, both), BF16),
            pltpu.VMEM((slots, width), BF16),
            pltpu.VMEM((chips, 2, down_rows, width), BF16),
            pltpu.VMEM((slots, hidden), BF16),
            pltpu.VMEM((slots, hidden), F32),
            pltpu.VMEM((slots, hidden), F32),
            pltpu.VMEM((n_dp, wide, both), BF16),
            pltpu.SemaphoreType.DMA((6,)),
            pltpu.SemaphoreType.DMA((5,)),
        ],
        compiler_params=params(50),
        cost_estimate=pl.CostEstimate(flops=6 * slots * hidden * width, bytes_accessed=6 * hidden * width, transcendentals=0),
        name="mid",
    )(mine, got, own_down, other_down, hid, slope, silu, packs)
    scaled, _ = lax.optimization_barrier((scaled, back))
    keep, give = pl.pallas_call(
        down_kernel,
        out_shape=(shape((hidden // 2, width)), shape((hidden // 2, width))),
        in_specs=[whole(pltpu.SMEM), whole(), whole()],
        out_specs=(whole(), whole()),
        compiler_params=params(20),
        cost_estimate=pl.CostEstimate(flops=2 * slots * hidden * width, bytes_accessed=2 * (slots + hidden) * width, transcendentals=0),
        name="down",
    )(mine, scaled, turned)
    taken = lax.ppermute(give, "dp", swap)
    chip_part = (keep.astype(F32) + taken.astype(F32)).astype(BF16)
    down_grad = lax.psum_scatter(
        chip_part,
        "dp",
        scatter_dimension=0,
        tiled=True,
        axis_index_groups=[list(range(c, n_dp, 2)) for c in range(2)],
    )
    back = exchange(back.reshape(dests, per, full), axes, near).reshape(slots, full)
    back, _ = lax.optimization_barrier((back, chip_part))
    place = (me // 2 // STRIDE).reshape(1).astype(jnp.int32)
    cut = (full // META + 1) // 2 * META
    own, after, left, right, before = pl.pallas_call(
        combine_kernel,
        out_shape=(
            shape((tok, full), F32),
            shape((tok, full), F32),
            shape((tok, cut)),
            shape((tok, full - cut)),
            shape((tok, full), F32),
        ),
        in_specs=[whole(pltpu.SMEM), whole(), whole()],
        out_specs=(whole(),) * 5,
        scratch_shapes=[pltpu.VMEM((STRIDE * tok, full), F32)],
        compiler_params=params(12),
        name="combine",
    )(place, select, back)

    def hop(value, step):
        perm = [(e, ((e // 2 + step) % n_z) * 2 + e % 2) for e in range(n_expert)]
        return lax.ppermute(value, "expert", perm)

    parts = [own]
    for name, part, piece, base, step in (("up", after, left, 0, STRIDE), ("down", before, right, cut, -STRIDE)):
        out = pl.pallas_call(
            functools.partial(pass_kernel, base),
            out_shape=shape((tok, full)),
            in_specs=[whole(), whole()],
            out_specs=whole(),
            compiler_params=params(8),
            name="pass_" + name,
        )(part, hop(piece, step))
        parts.append(hop(out, step))
    token_grad, route_grad = pl.pallas_call(
        last_kernel,
        out_shape=(shape((tok, width)), shape(expert_ids.shape[::-1])),
        in_specs=[whole()] * (1 + len(parts)),
        out_specs=(whole(), whole()),
        compiler_params=params(8),
        name="last",
    )(expert_ids.T, *parts)
    return token_grad, route_grad.T, down_grad[None]


def solution(mesh):
    return jax.shard_map(
        functools.partial(per_device, mesh.shape["dp"], mesh.shape["expert"]),
        mesh=mesh,
        in_specs=(
            P(("dp", "expert"), None),
            P(("dp", "expert"), None),
            P(("dp", "expert"), None),
            P("dp", "expert", None, None),
            P("expert", "dp", None),
            P("expert", "dp", None),
            P("expert", "dp", None),
        ),
        out_specs=(P(("dp", "expert"), None), P(("dp", "expert"), None), P("expert", "dp", None)),
        check_vma=False,
    )
```

```python
import functools

import jax
import jax.numpy as jnp
from jax import lax
from jax.experimental import pallas as pl
from jax.experimental.pallas import tpu as pltpu
from jax.sharding import PartitionSpec as P

BF16, F32 = jnp.bfloat16, jnp.float32
META = 128
STRIDE = 4


def params(mib):
    return pltpu.CompilerParams(vmem_limit_bytes=mib * 1024 * 1024)


def turn(values):
    rows, columns = values.shape
    if columns < META:
        values = jnp.concatenate([values, jnp.zeros((rows, META - columns), F32)], axis=1)
    if rows < META:
        values = jnp.concatenate([values, jnp.zeros((META - rows, META), F32)], axis=0)
    return values.T[:columns, :rows] if columns < META else values.T[:, :rows]


def even_first(hidden, rows):
    src = lax.broadcasted_iota(jnp.int32, (hidden, hidden), 0)
    at = lax.broadcasted_iota(jnp.int32, (1, hidden), 1)
    half = hidden // 2
    want = (2 * (at % half // rows) + at // half) * rows + at % rows
    return (src == want).astype(BF16)


def prep_kernel(
    rows_ref, ids_ref, weight_ref, gate_ref, up_ref, down_ref, tok_ref, pack_ref, downs_ref,
    tok_buf, gate_buf, up_buf, pack_buf, down_buf, ids_buf, weight_buf, in_sems, out_sems,
):
    tok, width = rows_ref.shape
    topk = ids_ref.shape[0]
    hidden = gate_ref.shape[1]
    copies = [
        pltpu.make_async_copy(ids_ref, ids_buf, in_sems.at[0]),
        pltpu.make_async_copy(weight_ref, weight_buf, in_sems.at[1]),
        pltpu.make_async_copy(down_ref, down_buf, in_sems.at[2]),
        pltpu.make_async_copy(rows_ref, tok_buf.at[:, pl.ds(0, width)], in_sems.at[3]),
        pltpu.make_async_copy(gate_ref, gate_buf, in_sems.at[4]),
        pltpu.make_async_copy(up_ref, up_buf, in_sems.at[5]),
    ]
    for copy in copies:
        copy.start()
    copies[0].wait()
    copies[1].wait()
    meta = jnp.concatenate([ids_buf[...].astype(F32), weight_buf[...].astype(F32)], axis=0)
    meta = jnp.concatenate([meta, jnp.zeros((META - 2 * topk, tok), F32)], axis=0)
    tok_buf[:, width:] = turn(meta).astype(BF16)
    copies[2].wait()
    outs = [
        pltpu.make_async_copy(down_buf, downs_ref.at[i], out_sems.at[2 + i]) for i in range(downs_ref.shape[0])
    ]
    for copy in outs:
        copy.start()
    copies[3].wait()
    outs.append(pltpu.make_async_copy(tok_buf, tok_ref, out_sems.at[0]))
    outs[-1].start()
    order = even_first(hidden, down_ref.shape[0])
    copies[4].wait()
    pack_buf[:, :hidden] = jnp.dot(gate_buf[...], order, preferred_element_type=F32).astype(BF16)
    copies[5].wait()
    pack_buf[:, hidden:] = jnp.dot(up_buf[...], order, preferred_element_type=F32).astype(BF16)
    outs.append(pltpu.make_async_copy(pack_buf, pack_ref, out_sems.at[1]))
    outs[-1].start()
    for copy in outs:
        copy.wait()


def select_kernel(cap, mine_ref, tok_ref, send_ref, select_ref):
    rows, full = tok_ref.shape
    width = full - META
    dests, per, _ = send_ref.shape
    block = rows // STRIDE
    topk = 8
    ids = tok_ref[:, width:].astype(F32).T[0:topk, :]
    member = jnp.concatenate(
        [
            jnp.max((ids == mine_ref[j].astype(F32)).astype(F32), axis=0, keepdims=True)
            for j in range(dests)
        ],
        axis=0,
    )
    before = lax.broadcasted_iota(jnp.int32, (rows, rows), 0)
    after = lax.broadcasted_iota(jnp.int32, (rows, rows), 1)
    earlier = (before < after) & (before // block == after // block)
    rank = jnp.dot(member.astype(BF16), earlier.astype(BF16), preferred_element_type=F32)
    key = jnp.where(member > 0.0, rank, -1.0)
    place = lax.broadcasted_iota(jnp.int32, (per, rows), 0)
    source = lax.broadcasted_iota(jnp.int32, (per, rows), 1) // block
    pattern = jnp.where(place // cap == source, place - source * cap, -2).astype(F32)
    for j in range(dests):
        chosen = (key[j : j + 1, :] == pattern).astype(BF16)
        select_ref[j * per : (j + 1) * per, :] = chosen
    sent = jnp.dot(select_ref[...], tok_ref[...], preferred_element_type=F32).astype(BF16)
    send_ref[...] = sent.reshape(send_ref.shape)


def act_kernel(cap, rows, pre_ref, hid_ref, turned_ref, slope_ref, silu_ref):
    slots, both = pre_ref.shape
    hidden = both // 2
    dests = slots // (cap * STRIDE)
    at = lax.broadcasted_iota(jnp.int32, (slots, slots), 0)
    src = lax.broadcasted_iota(jnp.int32, (slots, slots), 1)
    j, rest = at // (STRIDE * cap), at % (STRIDE * cap)
    k, r = rest // cap, rest % cap
    order = (src == (k * dests + j) * cap + r).astype(BF16)
    columns = even_first(hidden, rows)
    a, u = (
        jnp.dot(
            jnp.dot(order, part, preferred_element_type=F32).astype(BF16), columns, preferred_element_type=F32
        )
        for part in (pre_ref[:, :hidden], pre_ref[:, hidden:])
    )
    sig = jax.nn.sigmoid(a)
    silu = a * sig
    hid = (silu * u).astype(BF16)
    hid_ref[...] = hid
    turned_ref[...] = hid.astype(F32).T.astype(BF16)
    slope_ref[...] = u * sig * (1.0 + a * (1.0 - sig))
    silu_ref[...] = silu


def slot_weight(meta, expert):
    topk = 8
    meta = meta.astype(F32)
    lane = lax.broadcasted_iota(jnp.int32, meta.shape, 1)
    weight = pltpu.roll(meta, META - topk, 1)
    return jnp.sum(jnp.where((lane < topk) & (meta == expert.astype(F32)), weight, 0.0), axis=1, keepdims=True)


def down_kernel(mine_ref, scaled_ref, turned_ref, keep_ref, send_ref):
    half, width = keep_ref.shape
    core = mine_ref[1]
    columns = 512
    for at in range(0, width, columns):
        for ref, which in ((send_ref, 1 - core), (keep_ref, core)):
            begin = pl.multiple_of(which * half, half)
            ref[:, at : at + columns] = jnp.dot(
                turned_ref[pl.ds(begin, half), :], scaled_ref[:, at : at + columns], preferred_element_type=F32
            ).astype(BF16)


def mid_kernel(
    mine_ref, got_ref, own_ref, other_ref, hid_ref, slope_ref, silu_ref, pack_ref, out_ref, scaled_ref,
    out_buf, both_buf, scaled_buf, q_buf, wide_buf, in_sem, out_sems,
):
    width = got_ref.shape[1] - META
    hidden = hid_ref.shape[1]
    half = hidden // 2
    devices, wide, both = wide_buf.shape
    core = mine_ref[1]
    wide_copy = pltpu.make_async_copy(pack_ref, wide_buf, in_sem)
    wide_copy.start()
    w = slot_weight(got_ref[:, width:], mine_ref[0])
    scaled_buf[...] = (w * got_ref[:, :width].astype(F32)).astype(BF16)
    steps = out_sems.shape[0] - 1
    backs = [pltpu.make_async_copy(scaled_buf, scaled_ref, out_sems.at[steps])]
    backs[0].start()
    for ref, which in ((own_ref, core), (other_ref, 1 - core)):
        q_buf[:, pl.ds(pl.multiple_of(which * half, half), half)] = lax.dot_general(
            got_ref[:, :width],
            ref[...].reshape(half, width),
            (((1,), (1,)), ((), ())),
            preferred_element_type=F32,
        )
    q = q_buf[...]
    route = jnp.sum(q * hid_ref[...].astype(F32), axis=1, keepdims=True)
    grad = w * q
    both_buf[:, :hidden] = (grad * slope_ref[...]).astype(BF16)
    both_buf[:, hidden:] = (grad * silu_ref[...]).astype(BF16)
    lane = lax.broadcasted_iota(jnp.int32, (got_ref.shape[0], META), 1)
    out_buf[:, width:] = jnp.where(lane == mine_ref[0], route, 0.0).astype(BF16)
    wide_copy.wait()
    group = devices // steps
    for n in range(steps):
        at, size = n * group * wide, group * wide
        out_buf[:, at : at + size] = lax.dot_general(
            both_buf[...],
            wide_buf[n * group : (n + 1) * group].reshape(size, both),
            (((1,), (1,)), ((), ())),
            preferred_element_type=F32,
        ).astype(BF16)
        part = pl.ds(at, size + META if n == steps - 1 else size)
        backs.append(pltpu.make_async_copy(out_buf.at[:, part], out_ref.at[:, part], out_sems.at[n]))
        backs[-1].start()
    for copy in backs:
        copy.wait()


def combine_kernel(place_ref, select_ref, back_ref, own_ref, next_ref, left_ref, right_ref, before_ref, total_buf):
    tok = own_ref.shape[0]
    cut = left_ref.shape[1]
    total_buf[...] = lax.dot_general(
        select_ref[...], back_ref[...], (((0,), (0,)), ((), ())), preferred_element_type=F32
    )

    def rows(m):
        return pl.ds(pl.multiple_of(((place_ref[0] + m) % STRIDE) * tok, tok), tok)

    own_ref[...] = total_buf[rows(0), :]
    next_ref[...] = total_buf[rows(1), :]
    before_ref[...] = total_buf[rows(3), :]
    left_ref[...] = total_buf[rows(2), 0:cut].astype(BF16)
    right_ref[...] = total_buf[rows(2), cut:].astype(BF16)


def pass_kernel(base, part_ref, more_ref, out_ref):
    size = more_ref.shape[1]
    out_ref[...] = part_ref[...].astype(BF16)
    out_ref[:, base : base + size] = (part_ref[:, base : base + size] + more_ref[...].astype(F32)).astype(BF16)


def last_kernel(ids_ref, *refs):
    parts, (tok_ref, route_ref) = refs[:-2], refs[-2:]
    tok, width = tok_ref.shape
    total = parts[0][...]
    for ref in parts[1:]:
        total = total + ref[...].astype(F32)
    tok_ref[...] = total[:, :width].astype(BF16)
    route = turn(total[:, width:])
    ids = ids_ref[...]
    expert = lax.broadcasted_iota(jnp.int32, route.shape, 0)
    found = [
        jnp.sum(jnp.where(expert == ids[k : k + 1, :], route, 0.0), axis=0, keepdims=True)
        for k in range(ids.shape[0])
    ]
    route_ref[...] = jnp.concatenate(found, axis=0).astype(BF16)


def shape(dims, dtype=BF16):
    return jax.ShapeDtypeStruct(dims, dtype)


def whole(memory=pltpu.VMEM):
    return pl.BlockSpec(memory_space=memory)


def exchange(value, axes, groups):
    return lax.all_to_all(value, axes, 0, 0, axis_index_groups=groups, tiled=True)


def per_device(n_dp, n_expert, grad_out, expert_ids, route_weights, saved_pre, gate_weight, up_weight, down_weight):
    tok, width = grad_out.shape
    pre = saved_pre[0, 0]
    slots, both = pre.shape
    hidden = both // 2
    cap = slots // n_expert
    full = width + META
    n_z = n_expert // 2
    dests = slots // (cap * STRIDE)
    per = STRIDE * cap
    down_rows = down_weight.shape[1]
    axes = ("dp", "expert")

    apart = [
        [d * n_expert + (rho + STRIDE * k) * 2 + h for k in range(n_z // STRIDE)]
        for d in range(n_dp)
        for rho in range(STRIDE)
        for h in range(2)
    ]
    near = [
        [
            d * n_expert + ((STRIDE * a + (rho - 2 * (d % 2)) % STRIDE + 2 * (d % 2)) % n_z) * 2 + h
            for rho in range(STRIDE)
            for h in range(2)
        ]
        for d in range(n_dp)
        for a in range(n_z // STRIDE)
    ]
    core, me = lax.axis_index("dp") % 2, lax.axis_index("expert")
    shift = 2 * core
    quad = ((me // 2 - shift + n_z) % n_z) // STRIDE
    rho = jnp.arange(dests, dtype=jnp.int32) // 2
    members = ((STRIDE * quad + (rho - shift + STRIDE) % STRIDE + shift) % n_z) * 2 + jnp.arange(
        dests, dtype=jnp.int32
    ) % 2
    mine = jnp.stack([me, core]).astype(jnp.int32)

    wide = gate_weight.shape[1]
    chips = n_dp // 2
    rows, pack, downs = pl.pallas_call(
        prep_kernel,
        out_shape=(shape((tok, full)), shape((wide, both)), shape((chips, down_rows, width))),
        in_specs=[whole(pltpu.HBM)] * 6,
        out_specs=(whole(pltpu.HBM),) * 3,
        scratch_shapes=[
            pltpu.VMEM((tok, full), BF16),
            pltpu.VMEM((wide, hidden), BF16),
            pltpu.VMEM((wide, hidden), BF16),
            pltpu.VMEM((wide, both), BF16),
            pltpu.VMEM((down_rows, width), BF16),
            pltpu.VMEM((expert_ids.shape[1], tok), jnp.int32),
            pltpu.VMEM((expert_ids.shape[1], tok), BF16),
            pltpu.SemaphoreType.DMA((6,)),
            pltpu.SemaphoreType.DMA((2 + chips,)),
        ],
        compiler_params=params(60),
        name="prep",
    )(grad_out, expert_ids.T, route_weights.T, gate_weight[0], up_weight[0], down_weight[0])
    packs = lax.all_gather(pack, "dp", axis=0, tiled=False)
    same_core = [
        [d * n_expert + e for d in range(c, n_dp, 2)] for c in range(2) for e in range(n_expert)
    ]
    swap = [(d, d ^ 1) for d in range(n_dp)]
    own_down = exchange(downs, axes, same_core)
    blocks = lax.all_gather(rows, axes, axis=0, tiled=True, axis_index_groups=apart)
    send, select = pl.pallas_call(
        functools.partial(select_kernel, cap),
        out_shape=(shape((dests, per, full)), shape((slots, STRIDE * tok))),
        in_specs=[whole(pltpu.SMEM), whole()],
        out_specs=(whole(), whole()),
        compiler_params=params(16),
        name="select",
    )(members, blocks)
    own_down, send = lax.optimization_barrier((own_down, send))
    other_down = lax.ppermute(own_down, "dp", swap)
    got = exchange(send, axes, near).reshape(slots, full)
    hid, turned, slope, silu = pl.pallas_call(
        functools.partial(act_kernel, cap, down_rows),
        out_shape=(
            shape((slots, hidden)),
            shape((hidden, slots)),
            shape((slots, hidden), F32),
            shape((slots, hidden), F32),
        ),
        in_specs=[whole()],
        out_specs=(whole(),) * 4,
        compiler_params=params(24),
        cost_estimate=pl.CostEstimate(flops=slots * slots * both * 2, bytes_accessed=8 * slots * both, transcendentals=0),
        name="act",
    )(pre)
    back, scaled = pl.pallas_call(
        mid_kernel,
        out_shape=(shape((slots, full)), shape((slots, width))),
        in_specs=[whole(pltpu.SMEM)] + [whole()] * 6 + [whole(pltpu.HBM)],
        out_specs=(whole(pltpu.HBM),) * 2,
        scratch_shapes=[
            pltpu.VMEM((slots, full), BF16),
            pltpu.VMEM((slots, both), BF16),
            pltpu.VMEM((slots, width), BF16),
            pltpu.VMEM((slots, hidden), F32),
            pltpu.VMEM((n_dp, wide, both), BF16),
            pltpu.SemaphoreType.DMA,
            pltpu.SemaphoreType.DMA((5,)),
        ],
        compiler_params=params(50),
        cost_estimate=pl.CostEstimate(flops=6 * slots * hidden * width, bytes_accessed=6 * hidden * width, transcendentals=0),
        name="mid",
    )(mine, got, own_down, other_down, hid, slope, silu, packs)
    scaled, _ = lax.optimization_barrier((scaled, back))
    keep, give = pl.pallas_call(
        down_kernel,
        out_shape=(shape((hidden // 2, width)), shape((hidden // 2, width))),
        in_specs=[whole(pltpu.SMEM), whole(), whole()],
        out_specs=(whole(), whole()),
        compiler_params=params(20),
        cost_estimate=pl.CostEstimate(flops=2 * slots * hidden * width, bytes_accessed=2 * (slots + hidden) * width, transcendentals=0),
        name="down",
    )(mine, scaled, turned)
    taken = lax.ppermute(give, "dp", swap)
    chip_part = (keep.astype(F32) + taken.astype(F32)).astype(BF16)
    down_grad = lax.psum_scatter(
        chip_part,
        "dp",
        scatter_dimension=0,
        tiled=True,
        axis_index_groups=[list(range(c, n_dp, 2)) for c in range(2)],
    )
    back = exchange(back.reshape(dests, per, full), axes, near).reshape(slots, full)
    back, _ = lax.optimization_barrier((back, chip_part))
    place = (me // 2 // STRIDE).reshape(1).astype(jnp.int32)
    cut = (full // META + 1) // 2 * META
    own, after, left, right, before = pl.pallas_call(
        combine_kernel,
        out_shape=(
            shape((tok, full), F32),
            shape((tok, full), F32),
            shape((tok, cut)),
            shape((tok, full - cut)),
            shape((tok, full), F32),
        ),
        in_specs=[whole(pltpu.SMEM), whole(), whole()],
        out_specs=(whole(),) * 5,
        scratch_shapes=[pltpu.VMEM((STRIDE * tok, full), F32)],
        compiler_params=params(12),
        name="combine",
    )(place, select, back)

    def hop(value, step):
        perm = [(e, ((e // 2 + step) % n_z) * 2 + e % 2) for e in range(n_expert)]
        return lax.ppermute(value, "expert", perm)

    parts = [own]
    for name, part, piece, base, step in (("up", after, left, 0, STRIDE), ("down", before, right, cut, -STRIDE)):
        out = pl.pallas_call(
            functools.partial(pass_kernel, base),
            out_shape=shape((tok, full)),
            in_specs=[whole(), whole()],
            out_specs=whole(),
            compiler_params=params(8),
            name="pass_" + name,
        )(part, hop(piece, step))
        parts.append(hop(out, step))
    token_grad, route_grad = pl.pallas_call(
        last_kernel,
        out_shape=(shape((tok, width)), shape(expert_ids.shape[::-1])),
        in_specs=[whole()] * (1 + len(parts)),
        out_specs=(whole(), whole()),
        compiler_params=params(8),
        name="last",
    )(expert_ids.T, *parts)
    return token_grad, route_grad.T, down_grad[None]


def solution(mesh):
    return jax.shard_map(
        functools.partial(per_device, mesh.shape["dp"], mesh.shape["expert"]),
        mesh=mesh,
        in_specs=(
            P(("dp", "expert"), None),
            P(("dp", "expert"), None),
            P(("dp", "expert"), None),
            P("dp", "expert", None, None),
            P("expert", "dp", None),
            P("expert", "dp", None),
            P("expert", "dp", None),
        ),
        out_specs=(P(("dp", "expert"), None), P(("dp", "expert"), None), P("expert", "dp", None)),
        check_vma=False,
    )
```

```python
import functools

import jax
import jax.numpy as jnp
from jax import lax
from jax.experimental import pallas as pl
from jax.experimental.pallas import tpu as pltpu
from jax.sharding import PartitionSpec as P

BF16, F32 = jnp.bfloat16, jnp.float32
META = 128
STRIDE = 4


def params(mib):
    return pltpu.CompilerParams(vmem_limit_bytes=mib * 1024 * 1024)


def turn(values):
    rows, columns = values.shape
    if columns < META:
        values = jnp.concatenate([values, jnp.zeros((rows, META - columns), F32)], axis=1)
    if rows < META:
        values = jnp.concatenate([values, jnp.zeros((META - rows, META), F32)], axis=0)
    return values.T[:columns, :rows] if columns < META else values.T[:, :rows]


def prep_kernel(
    rows_ref, ids_ref, weight_ref, gate_ref, up_ref, down_ref, tok_ref, pack_ref, downs_ref,
    tok_buf, pack_buf, down_buf, in_sems, out_sems,
):
    tok, width = rows_ref.shape
    topk = ids_ref.shape[0]
    hidden = gate_ref.shape[1]
    copies = [
        pltpu.make_async_copy(down_ref, down_buf, in_sems.at[0]),
        pltpu.make_async_copy(rows_ref, tok_buf.at[:, pl.ds(0, width)], in_sems.at[1]),
        pltpu.make_async_copy(gate_ref, pack_buf.at[:, pl.ds(0, hidden)], in_sems.at[2]),
        pltpu.make_async_copy(up_ref, pack_buf.at[:, pl.ds(hidden, hidden)], in_sems.at[3]),
    ]
    for copy in copies:
        copy.start()
    meta = jnp.concatenate([ids_ref[...].astype(F32), weight_ref[...].astype(F32)], axis=0)
    meta = jnp.concatenate([meta, jnp.zeros((META - 2 * topk, tok), F32)], axis=0)
    tok_buf[:, width:] = turn(meta).astype(BF16)
    copies[0].wait()
    outs = [
        pltpu.make_async_copy(down_buf, downs_ref.at[i], out_sems.at[2 + i]) for i in range(downs_ref.shape[0])
    ]
    for copy in outs:
        copy.start()
    copies[1].wait()
    outs.append(pltpu.make_async_copy(tok_buf, tok_ref, out_sems.at[0]))
    outs[-1].start()
    copies[2].wait()
    copies[3].wait()
    outs.append(pltpu.make_async_copy(pack_buf, pack_ref, out_sems.at[1]))
    outs[-1].start()
    for copy in outs:
        copy.wait()


def select_kernel(cap, mine_ref, tok_ref, send_ref, select_ref, send_buf, sems):
    rows, full = tok_ref.shape
    width = full - META
    dests, per, _ = send_ref.shape
    block = rows // STRIDE
    topk = 8
    ids = tok_ref[:, width:].astype(F32).T[0:topk, :]
    member = jnp.concatenate(
        [
            jnp.max((ids == mine_ref[j].astype(F32)).astype(F32), axis=0, keepdims=True)
            for j in range(dests)
        ],
        axis=0,
    )
    before = lax.broadcasted_iota(jnp.int32, (rows, rows), 0)
    after = lax.broadcasted_iota(jnp.int32, (rows, rows), 1)
    earlier = (before < after) & (before // block == after // block)
    rank = jnp.dot(member.astype(BF16), earlier.astype(BF16), preferred_element_type=F32)
    key = jnp.where(member > 0.0, rank, -1.0)
    place = lax.broadcasted_iota(jnp.int32, (per, rows), 0)
    source = lax.broadcasted_iota(jnp.int32, (per, rows), 1) // block
    pattern = jnp.where(place // cap == source, place - source * cap, -2).astype(F32)
    for j in range(dests):
        chosen = (key[j : j + 1, :] == pattern).astype(BF16)
        select_ref[j * per : (j + 1) * per, :] = chosen
    cuts = [full * n // META // sems.shape[0] * META for n in range(sems.shape[0])] + [full]
    copies = []
    for n, (at, end) in enumerate(zip(cuts[:-1], cuts[1:])):
        sent = jnp.dot(select_ref[...], tok_ref[:, at:end], preferred_element_type=F32).astype(BF16)
        send_buf[:, :, at:end] = sent.reshape(dests, per, end - at)
        part = pl.ds(at, end - at)
        copies.append(pltpu.make_async_copy(send_buf.at[:, :, part], send_ref.at[:, :, part], sems.at[n]))
        copies[-1].start()
    for copy in copies:
        copy.wait()


def act_kernel(cap, rows, pre_ref, hid_ref, turned_ref, slope_ref, silu_ref):
    slots, both = pre_ref.shape
    hidden = both // 2
    dests = slots // (cap * STRIDE)
    at = lax.broadcasted_iota(jnp.int32, (slots, slots), 0)
    src = lax.broadcasted_iota(jnp.int32, (slots, slots), 1)
    j, rest = at // (STRIDE * cap), at % (STRIDE * cap)
    k, r = rest // cap, rest % cap
    order = (src == (k * dests + j) * cap + r).astype(BF16)
    a = jnp.dot(order, pre_ref[:, :hidden], preferred_element_type=F32)
    u = jnp.dot(order, pre_ref[:, hidden:], preferred_element_type=F32)
    sig = jax.nn.sigmoid(a)
    silu = a * sig
    hid = (silu * u).astype(BF16)
    hid_ref[...] = hid
    turned = hid.astype(F32).T.astype(BF16)
    for block in range(hidden // rows):
        at = (block % 2) * (hidden // 2) + (block // 2) * rows
        turned_ref[at : at + rows, :] = turned[block * rows : (block + 1) * rows]
    slope_ref[...] = u * sig * (1.0 + a * (1.0 - sig))
    silu_ref[...] = silu


def slot_weight(meta, expert):
    topk = 8
    meta = meta.astype(F32)
    lane = lax.broadcasted_iota(jnp.int32, meta.shape, 1)
    weight = pltpu.roll(meta, META - topk, 1)
    return jnp.sum(jnp.where((lane < topk) & (meta == expert.astype(F32)), weight, 0.0), axis=1, keepdims=True)


def down_kernel(mine_ref, scaled_ref, turned_ref, keep_ref, send_ref):
    half, width = keep_ref.shape
    core = mine_ref[1]
    columns = 512
    for at in range(0, width, columns):
        for ref, which in ((send_ref, 1 - core), (keep_ref, core)):
            begin = pl.multiple_of(which * half, half)
            ref[:, at : at + columns] = jnp.dot(
                turned_ref[pl.ds(begin, half), :], scaled_ref[:, at : at + columns], preferred_element_type=F32
            ).astype(BF16)


def mid_kernel(
    mine_ref, got_ref, own_ref, other_ref, hid_ref, slope_ref, silu_ref, pack_ref, out_ref, scaled_ref,
    out_buf, both_buf, scaled_buf, down_buf, hid_buf, slope_buf, silu_buf, wide_buf, in_sems, out_sems,
):
    width = got_ref.shape[1] - META
    hidden = hid_ref.shape[1]
    devices, wide, both = wide_buf.shape
    core = mine_ref[1]
    places = (
        (own_ref, down_buf.at[:, core]),
        (other_ref, down_buf.at[:, 1 - core]),
        (hid_ref, hid_buf),
        (slope_ref, slope_buf),
        (silu_ref, silu_buf),
        (pack_ref, wide_buf),
    )
    copies = [pltpu.make_async_copy(src, dst, in_sems.at[n]) for n, (src, dst) in enumerate(places)]
    for copy in copies:
        copy.start()
    w = slot_weight(got_ref[:, width:], mine_ref[0])
    scaled_buf[...] = (w * got_ref[:, :width].astype(F32)).astype(BF16)
    steps = out_sems.shape[0] - 1
    backs = [pltpu.make_async_copy(scaled_buf, scaled_ref, out_sems.at[steps])]
    backs[0].start()
    copies[0].wait()
    copies[1].wait()
    q = lax.dot_general(
        got_ref[:, :width],
        down_buf[...].reshape(hidden, width),
        (((1,), (1,)), ((), ())),
        preferred_element_type=F32,
    )
    for copy in copies[2:5]:
        copy.wait()
    route = jnp.sum(q * hid_buf[...].astype(F32), axis=1, keepdims=True)
    grad = w * q
    both_buf[:, :hidden] = (grad * slope_buf[...]).astype(BF16)
    both_buf[:, hidden:] = (grad * silu_buf[...]).astype(BF16)
    lane = lax.broadcasted_iota(jnp.int32, (got_ref.shape[0], META), 1)
    out_buf[:, width:] = jnp.where(lane == mine_ref[0], route, 0.0).astype(BF16)
    copies[5].wait()
    group = devices // steps
    for n in range(steps):
        at, size = n * group * wide, group * wide
        out_buf[:, at : at + size] = lax.dot_general(
            both_buf[...],
            wide_buf[n * group : (n + 1) * group].reshape(size, both),
            (((1,), (1,)), ((), ())),
            preferred_element_type=F32,
        ).astype(BF16)
        part = pl.ds(at, size + META if n == steps - 1 else size)
        backs.append(pltpu.make_async_copy(out_buf.at[:, part], out_ref.at[:, part], out_sems.at[n]))
        backs[-1].start()
    for copy in backs:
        copy.wait()


def combine_kernel(place_ref, select_ref, back_ref, own_ref, next_ref, left_ref, right_ref, before_ref, total_buf):
    tok = own_ref.shape[0]
    cut = left_ref.shape[1]
    total_buf[...] = lax.dot_general(
        select_ref[...], back_ref[...], (((0,), (0,)), ((), ())), preferred_element_type=F32
    )

    def rows(m):
        return pl.ds(pl.multiple_of(((place_ref[0] + m) % STRIDE) * tok, tok), tok)

    own_ref[...] = total_buf[rows(0), :]
    next_ref[...] = total_buf[rows(1), :]
    before_ref[...] = total_buf[rows(3), :]
    left_ref[...] = total_buf[rows(2), 0:cut].astype(BF16)
    right_ref[...] = total_buf[rows(2), cut:].astype(BF16)


def pass_kernel(base, part_ref, more_ref, out_ref):
    size = more_ref.shape[1]
    out_ref[...] = part_ref[...].astype(BF16)
    out_ref[:, base : base + size] = (part_ref[:, base : base + size] + more_ref[...].astype(F32)).astype(BF16)


def last_kernel(ids_ref, *refs):
    parts, (tok_ref, route_ref) = refs[:-2], refs[-2:]
    tok, width = tok_ref.shape
    total = parts[0][...]
    for ref in parts[1:]:
        total = total + ref[...].astype(F32)
    tok_ref[...] = total[:, :width].astype(BF16)
    route = turn(total[:, width:])
    ids = ids_ref[...]
    expert = lax.broadcasted_iota(jnp.int32, route.shape, 0)
    found = [
        jnp.sum(jnp.where(expert == ids[k : k + 1, :], route, 0.0), axis=0, keepdims=True)
        for k in range(ids.shape[0])
    ]
    route_ref[...] = jnp.concatenate(found, axis=0).astype(BF16)


def shape(dims, dtype=BF16):
    return jax.ShapeDtypeStruct(dims, dtype)


def whole(memory=pltpu.VMEM):
    return pl.BlockSpec(memory_space=memory)


def exchange(value, axes, groups):
    return lax.all_to_all(value, axes, 0, 0, axis_index_groups=groups, tiled=True)


def per_device(n_dp, n_expert, grad_out, expert_ids, route_weights, saved_pre, gate_weight, up_weight, down_weight):
    tok, width = grad_out.shape
    pre = saved_pre[0, 0]
    slots, both = pre.shape
    hidden = both // 2
    cap = slots // n_expert
    full = width + META
    n_z = n_expert // 2
    dests = slots // (cap * STRIDE)
    per = STRIDE * cap
    down_rows = down_weight.shape[1]
    axes = ("dp", "expert")

    apart = [
        [d * n_expert + (rho + STRIDE * k) * 2 + h for k in range(n_z // STRIDE)]
        for d in range(n_dp)
        for rho in range(STRIDE)
        for h in range(2)
    ]
    near = [
        [
            d * n_expert + ((STRIDE * a + (rho - 2 * (d % 2)) % STRIDE + 2 * (d % 2)) % n_z) * 2 + h
            for rho in range(STRIDE)
            for h in range(2)
        ]
        for d in range(n_dp)
        for a in range(n_z // STRIDE)
    ]
    core, me = lax.axis_index("dp") % 2, lax.axis_index("expert")
    shift = 2 * core
    quad = ((me // 2 - shift + n_z) % n_z) // STRIDE
    rho = jnp.arange(dests, dtype=jnp.int32) // 2
    members = ((STRIDE * quad + (rho - shift + STRIDE) % STRIDE + shift) % n_z) * 2 + jnp.arange(
        dests, dtype=jnp.int32
    ) % 2
    mine = jnp.stack([me, core]).astype(jnp.int32)

    wide = gate_weight.shape[1]
    chips = n_dp // 2
    rows, pack, downs = pl.pallas_call(
        prep_kernel,
        out_shape=(shape((tok, full)), shape((wide, both)), shape((chips, down_rows, width))),
        in_specs=[whole(pltpu.HBM), whole(), whole()] + [whole(pltpu.HBM)] * 3,
        out_specs=(whole(pltpu.HBM),) * 3,
        scratch_shapes=[
            pltpu.VMEM((tok, full), BF16),
            pltpu.VMEM((wide, both), BF16),
            pltpu.VMEM((down_rows, width), BF16),
            pltpu.SemaphoreType.DMA((4,)),
            pltpu.SemaphoreType.DMA((2 + chips,)),
        ],
        compiler_params=params(60),
        name="prep",
    )(grad_out, expert_ids.T, route_weights.T, gate_weight[0], up_weight[0], down_weight[0])
    packs = lax.all_gather(pack, "dp", axis=0, tiled=False)
    same_core = [
        [d * n_expert + e for d in range(c, n_dp, 2)] for c in range(2) for e in range(n_expert)
    ]
    swap = [(d, d ^ 1) for d in range(n_dp)]
    own_down = exchange(downs, axes, same_core)
    blocks = lax.all_gather(rows, axes, axis=0, tiled=True, axis_index_groups=apart)
    send, select = pl.pallas_call(
        functools.partial(select_kernel, cap),
        out_shape=(shape((dests, per, full)), shape((slots, STRIDE * tok))),
        in_specs=[whole(pltpu.SMEM), whole()],
        out_specs=(whole(pltpu.HBM), whole()),
        scratch_shapes=[pltpu.VMEM((dests, per, full), BF16), pltpu.SemaphoreType.DMA((3,))],
        compiler_params=params(16),
        name="select",
    )(members, blocks)
    own_down, send = lax.optimization_barrier((own_down, send))
    other_down = lax.ppermute(own_down, "dp", swap)
    got = exchange(send, axes, near).reshape(slots, full)
    hid, turned, slope, silu = pl.pallas_call(
        functools.partial(act_kernel, cap, down_rows),
        out_shape=(
            shape((slots, hidden)),
            shape((hidden, slots)),
            shape((slots, hidden), F32),
            shape((slots, hidden), F32),
        ),
        in_specs=[whole()],
        out_specs=(whole(),) * 4,
        compiler_params=params(24),
        cost_estimate=pl.CostEstimate(flops=slots * slots * both * 2, bytes_accessed=8 * slots * both, transcendentals=0),
        name="act",
    )(pre)
    back, scaled = pl.pallas_call(
        mid_kernel,
        out_shape=(shape((slots, full)), shape((slots, width))),
        in_specs=[whole(pltpu.SMEM), whole()] + [whole(pltpu.HBM)] * 6,
        out_specs=(whole(pltpu.HBM),) * 2,
        scratch_shapes=[
            pltpu.VMEM((slots, full), BF16),
            pltpu.VMEM((slots, both), BF16),
            pltpu.VMEM((slots, width), BF16),
            pltpu.VMEM((chips, 2, down_rows, width), BF16),
            pltpu.VMEM((slots, hidden), BF16),
            pltpu.VMEM((slots, hidden), F32),
            pltpu.VMEM((slots, hidden), F32),
            pltpu.VMEM((n_dp, wide, both), BF16),
            pltpu.SemaphoreType.DMA((6,)),
            pltpu.SemaphoreType.DMA((5,)),
        ],
        compiler_params=params(50),
        cost_estimate=pl.CostEstimate(flops=6 * slots * hidden * width, bytes_accessed=6 * hidden * width, transcendentals=0),
        name="mid",
    )(mine, got, own_down, other_down, hid, slope, silu, packs)
    scaled, _ = lax.optimization_barrier((scaled, back))
    keep, give = pl.pallas_call(
        down_kernel,
        out_shape=(shape((hidden // 2, width)), shape((hidden // 2, width))),
        in_specs=[whole(pltpu.SMEM), whole(), whole()],
        out_specs=(whole(), whole()),
        compiler_params=params(20),
        cost_estimate=pl.CostEstimate(flops=2 * slots * hidden * width, bytes_accessed=2 * (slots + hidden) * width, transcendentals=0),
        name="down",
    )(mine, scaled, turned)
    taken = lax.ppermute(give, "dp", swap)
    chip_part = (keep.astype(F32) + taken.astype(F32)).astype(BF16)
    down_grad = lax.psum_scatter(
        chip_part,
        "dp",
        scatter_dimension=0,
        tiled=True,
        axis_index_groups=[list(range(c, n_dp, 2)) for c in range(2)],
    )
    back = exchange(back.reshape(dests, per, full), axes, near).reshape(slots, full)
    back, _ = lax.optimization_barrier((back, chip_part))
    place = (me // 2 // STRIDE).reshape(1).astype(jnp.int32)
    cut = (full // META + 1) // 2 * META
    own, after, left, right, before = pl.pallas_call(
        combine_kernel,
        out_shape=(
            shape((tok, full), F32),
            shape((tok, full), F32),
            shape((tok, cut)),
            shape((tok, full - cut)),
            shape((tok, full), F32),
        ),
        in_specs=[whole(pltpu.SMEM), whole(), whole()],
        out_specs=(whole(),) * 5,
        scratch_shapes=[pltpu.VMEM((STRIDE * tok, full), F32)],
        compiler_params=params(12),
        name="combine",
    )(place, select, back)

    def hop(value, step):
        perm = [(e, ((e // 2 + step) % n_z) * 2 + e % 2) for e in range(n_expert)]
        return lax.ppermute(value, "expert", perm)

    parts = [own]
    for name, part, piece, base, step in (("up", after, left, 0, STRIDE), ("down", before, right, cut, -STRIDE)):
        out = pl.pallas_call(
            functools.partial(pass_kernel, base),
            out_shape=shape((tok, full)),
            in_specs=[whole(), whole()],
            out_specs=whole(),
            compiler_params=params(8),
            name="pass_" + name,
        )(part, hop(piece, step))
        parts.append(hop(out, step))
    token_grad, route_grad = pl.pallas_call(
        last_kernel,
        out_shape=(shape((tok, width)), shape(expert_ids.shape[::-1])),
        in_specs=[whole()] * (1 + len(parts)),
        out_specs=(whole(), whole()),
        compiler_params=params(8),
        name="last",
    )(expert_ids.T, *parts)
    return token_grad, route_grad.T, down_grad[None]


def solution(mesh):
    return jax.shard_map(
        functools.partial(per_device, mesh.shape["dp"], mesh.shape["expert"]),
        mesh=mesh,
        in_specs=(
            P(("dp", "expert"), None),
            P(("dp", "expert"), None),
            P(("dp", "expert"), None),
            P("dp", "expert", None, None),
            P("expert", "dp", None),
            P("expert", "dp", None),
            P("expert", "dp", None),
        ),
        out_specs=(P(("dp", "expert"), None), P(("dp", "expert"), None), P("expert", "dp", None)),
        check_vma=False,
    )
```

```python
import functools

import jax
import jax.numpy as jnp
from jax import lax
from jax.experimental import pallas as pl
from jax.experimental.pallas import tpu as pltpu
from jax.sharding import PartitionSpec as P

BF16, F32 = jnp.bfloat16, jnp.float32
META = 128
STRIDE = 4


def params(mib):
    return pltpu.CompilerParams(vmem_limit_bytes=mib * 1024 * 1024)


def turn(values):
    rows, columns = values.shape
    if columns < META:
        values = jnp.concatenate([values, jnp.zeros((rows, META - columns), F32)], axis=1)
    if rows < META:
        values = jnp.concatenate([values, jnp.zeros((META - rows, META), F32)], axis=0)
    return values.T[:columns, :rows] if columns < META else values.T[:, :rows]


def prep_kernel(
    rows_ref, ids_ref, weight_ref, gate_ref, up_ref, down_ref, tok_ref, pack_ref, downs_ref,
    tok_buf, pack_buf, down_buf, ids_buf, weight_buf, in_sems, out_sems,
):
    tok, width = rows_ref.shape
    topk = ids_ref.shape[0]
    hidden = gate_ref.shape[1]
    copies = [
        pltpu.make_async_copy(ids_ref, ids_buf, in_sems.at[0]),
        pltpu.make_async_copy(weight_ref, weight_buf, in_sems.at[1]),
        pltpu.make_async_copy(down_ref, down_buf, in_sems.at[2]),
        pltpu.make_async_copy(rows_ref, tok_buf.at[:, pl.ds(0, width)], in_sems.at[3]),
        pltpu.make_async_copy(gate_ref, pack_buf.at[:, pl.ds(0, hidden)], in_sems.at[4]),
        pltpu.make_async_copy(up_ref, pack_buf.at[:, pl.ds(hidden, hidden)], in_sems.at[5]),
    ]
    for copy in copies:
        copy.start()
    copies[0].wait()
    copies[1].wait()
    meta = jnp.concatenate([ids_buf[...].astype(F32), weight_buf[...].astype(F32)], axis=0)
    meta = jnp.concatenate([meta, jnp.zeros((META - 2 * topk, tok), F32)], axis=0)
    tok_buf[:, width:] = turn(meta).astype(BF16)
    copies[2].wait()
    outs = [
        pltpu.make_async_copy(down_buf, downs_ref.at[i], out_sems.at[2 + i]) for i in range(downs_ref.shape[0])
    ]
    for copy in outs:
        copy.start()
    copies[3].wait()
    outs.append(pltpu.make_async_copy(tok_buf, tok_ref, out_sems.at[0]))
    outs[-1].start()
    copies[4].wait()
    copies[5].wait()
    outs.append(pltpu.make_async_copy(pack_buf, pack_ref, out_sems.at[1]))
    outs[-1].start()
    for copy in outs:
        copy.wait()


def select_kernel(cap, mine_ref, tok_ref, send_ref, select_ref, send_buf, sems):
    rows, full = tok_ref.shape
    width = full - META
    dests, per, _ = send_ref.shape
    block = rows // STRIDE
    topk = 8
    ids = tok_ref[:, width:].astype(F32).T[0:topk, :]
    member = jnp.concatenate(
        [
            jnp.max((ids == mine_ref[j].astype(F32)).astype(F32), axis=0, keepdims=True)
            for j in range(dests)
        ],
        axis=0,
    )
    before = lax.broadcasted_iota(jnp.int32, (rows, rows), 0)
    after = lax.broadcasted_iota(jnp.int32, (rows, rows), 1)
    earlier = (before < after) & (before // block == after // block)
    rank = jnp.dot(member.astype(BF16), earlier.astype(BF16), preferred_element_type=F32)
    key = jnp.where(member > 0.0, rank, -1.0)
    place = lax.broadcasted_iota(jnp.int32, (per, rows), 0)
    source = lax.broadcasted_iota(jnp.int32, (per, rows), 1) // block
    pattern = jnp.where(place // cap == source, place - source * cap, -2).astype(F32)
    for j in range(dests):
        chosen = (key[j : j + 1, :] == pattern).astype(BF16)
        select_ref[j * per : (j + 1) * per, :] = chosen
    cuts = [full * n // META // sems.shape[0] * META for n in range(sems.shape[0])] + [full]
    copies = []
    for n, (at, end) in enumerate(zip(cuts[:-1], cuts[1:])):
        sent = jnp.dot(select_ref[...], tok_ref[:, at:end], preferred_element_type=F32).astype(BF16)
        send_buf[:, :, at:end] = sent.reshape(dests, per, end - at)
        part = pl.ds(at, end - at)
        copies.append(pltpu.make_async_copy(send_buf.at[:, :, part], send_ref.at[:, :, part], sems.at[n]))
        copies[-1].start()
    for copy in copies:
        copy.wait()


def act_kernel(cap, rows, pre_ref, hid_ref, turned_ref, slope_ref, silu_ref):
    slots, both = pre_ref.shape
    hidden = both // 2
    dests = slots // (cap * STRIDE)
    at = lax.broadcasted_iota(jnp.int32, (slots, slots), 0)
    src = lax.broadcasted_iota(jnp.int32, (slots, slots), 1)
    j, rest = at // (STRIDE * cap), at % (STRIDE * cap)
    k, r = rest // cap, rest % cap
    order = (src == (k * dests + j) * cap + r).astype(BF16)
    a = jnp.dot(order, pre_ref[:, :hidden], preferred_element_type=F32)
    u = jnp.dot(order, pre_ref[:, hidden:], preferred_element_type=F32)
    sig = jax.nn.sigmoid(a)
    silu = a * sig
    hid = (silu * u).astype(BF16)
    hid_ref[...] = hid
    turned = hid.astype(F32).T.astype(BF16)
    for block in range(hidden // rows):
        at = (block % 2) * (hidden // 2) + (block // 2) * rows
        turned_ref[at : at + rows, :] = turned[block * rows : (block + 1) * rows]
    slope_ref[...] = u * sig * (1.0 + a * (1.0 - sig))
    silu_ref[...] = silu


def slot_weight(meta, expert):
    topk = 8
    meta = meta.astype(F32)
    lane = lax.broadcasted_iota(jnp.int32, meta.shape, 1)
    weight = pltpu.roll(meta, META - topk, 1)
    return jnp.sum(jnp.where((lane < topk) & (meta == expert.astype(F32)), weight, 0.0), axis=1, keepdims=True)


def down_kernel(mine_ref, scaled_ref, turned_ref, keep_ref, send_ref):
    half, width = keep_ref.shape
    core = mine_ref[1]
    columns = 512
    for at in range(0, width, columns):
        for ref, which in ((send_ref, 1 - core), (keep_ref, core)):
            begin = pl.multiple_of(which * half, half)
            ref[:, at : at + columns] = jnp.dot(
                turned_ref[pl.ds(begin, half), :], scaled_ref[:, at : at + columns], preferred_element_type=F32
            ).astype(BF16)


def mid_kernel(
    mine_ref, got_ref, own_ref, other_ref, hid_ref, slope_ref, silu_ref, pack_ref, out_ref, scaled_ref,
    out_buf, both_buf, scaled_buf, down_buf, hid_buf, slope_buf, silu_buf, wide_buf, in_sems, out_sems,
):
    width = got_ref.shape[1] - META
    hidden = hid_ref.shape[1]
    devices, wide, both = wide_buf.shape
    core = mine_ref[1]
    places = (
        (own_ref, down_buf.at[:, core]),
        (other_ref, down_buf.at[:, 1 - core]),
        (hid_ref, hid_buf),
        (slope_ref, slope_buf),
        (silu_ref, silu_buf),
        (pack_ref, wide_buf),
    )
    copies = [pltpu.make_async_copy(src, dst, in_sems.at[n]) for n, (src, dst) in enumerate(places)]
    for copy in copies:
        copy.start()
    w = slot_weight(got_ref[:, width:], mine_ref[0])
    scaled_buf[...] = (w * got_ref[:, :width].astype(F32)).astype(BF16)
    steps = out_sems.shape[0] - 1
    backs = [pltpu.make_async_copy(scaled_buf, scaled_ref, out_sems.at[steps])]
    backs[0].start()
    copies[0].wait()
    copies[1].wait()
    q = lax.dot_general(
        got_ref[:, :width],
        down_buf[...].reshape(hidden, width),
        (((1,), (1,)), ((), ())),
        preferred_element_type=F32,
    )
    for copy in copies[2:5]:
        copy.wait()
    route = jnp.sum(q * hid_buf[...].astype(F32), axis=1, keepdims=True)
    grad = w * q
    both_buf[:, :hidden] = (grad * slope_buf[...]).astype(BF16)
    both_buf[:, hidden:] = (grad * silu_buf[...]).astype(BF16)
    lane = lax.broadcasted_iota(jnp.int32, (got_ref.shape[0], META), 1)
    out_buf[:, width:] = jnp.where(lane == mine_ref[0], route, 0.0).astype(BF16)
    copies[5].wait()
    group = devices // steps
    for n in range(steps):
        at, size = n * group * wide, group * wide
        out_buf[:, at : at + size] = lax.dot_general(
            both_buf[...],
            wide_buf[n * group : (n + 1) * group].reshape(size, both),
            (((1,), (1,)), ((), ())),
            preferred_element_type=F32,
        ).astype(BF16)
        part = pl.ds(at, size + META if n == steps - 1 else size)
        backs.append(pltpu.make_async_copy(out_buf.at[:, part], out_ref.at[:, part], out_sems.at[n]))
        backs[-1].start()
    for copy in backs:
        copy.wait()


def combine_kernel(place_ref, select_ref, back_ref, own_ref, next_ref, left_ref, right_ref, before_ref, total_buf):
    tok = own_ref.shape[0]
    cut = left_ref.shape[1]
    total_buf[...] = lax.dot_general(
        select_ref[...], back_ref[...], (((0,), (0,)), ((), ())), preferred_element_type=F32
    )

    def rows(m):
        return pl.ds(pl.multiple_of(((place_ref[0] + m) % STRIDE) * tok, tok), tok)

    own_ref[...] = total_buf[rows(0), :]
    next_ref[...] = total_buf[rows(1), :]
    before_ref[...] = total_buf[rows(3), :]
    left_ref[...] = total_buf[rows(2), 0:cut].astype(BF16)
    right_ref[...] = total_buf[rows(2), cut:].astype(BF16)


def pass_kernel(base, part_ref, more_ref, out_ref):
    size = more_ref.shape[1]
    out_ref[...] = part_ref[...].astype(BF16)
    out_ref[:, base : base + size] = (part_ref[:, base : base + size] + more_ref[...].astype(F32)).astype(BF16)


def last_kernel(ids_ref, *refs):
    parts, (tok_ref, route_ref) = refs[:-2], refs[-2:]
    tok, width = tok_ref.shape
    total = parts[0][...]
    for ref in parts[1:]:
        total = total + ref[...].astype(F32)
    tok_ref[...] = total[:, :width].astype(BF16)
    route = turn(total[:, width:])
    ids = ids_ref[...]
    expert = lax.broadcasted_iota(jnp.int32, route.shape, 0)
    found = [
        jnp.sum(jnp.where(expert == ids[k : k + 1, :], route, 0.0), axis=0, keepdims=True)
        for k in range(ids.shape[0])
    ]
    route_ref[...] = jnp.concatenate(found, axis=0).astype(BF16)


def shape(dims, dtype=BF16):
    return jax.ShapeDtypeStruct(dims, dtype)


def whole(memory=pltpu.VMEM):
    return pl.BlockSpec(memory_space=memory)


def exchange(value, axes, groups):
    return lax.all_to_all(value, axes, 0, 0, axis_index_groups=groups, tiled=True)


def per_device(n_dp, n_expert, grad_out, expert_ids, route_weights, saved_pre, gate_weight, up_weight, down_weight):
    tok, width = grad_out.shape
    pre = saved_pre[0, 0]
    slots, both = pre.shape
    hidden = both // 2
    cap = slots // n_expert
    full = width + META
    n_z = n_expert // 2
    dests = slots // (cap * STRIDE)
    per = STRIDE * cap
    down_rows = down_weight.shape[1]
    axes = ("dp", "expert")

    apart = [
        [d * n_expert + (rho + STRIDE * k) * 2 + h for k in range(n_z // STRIDE)]
        for d in range(n_dp)
        for rho in range(STRIDE)
        for h in range(2)
    ]
    near = [
        [
            d * n_expert + ((STRIDE * a + (rho - 2 * (d % 2)) % STRIDE + 2 * (d % 2)) % n_z) * 2 + h
            for rho in range(STRIDE)
            for h in range(2)
        ]
        for d in range(n_dp)
        for a in range(n_z // STRIDE)
    ]
    core, me = lax.axis_index("dp") % 2, lax.axis_index("expert")
    shift = 2 * core
    quad = ((me // 2 - shift + n_z) % n_z) // STRIDE
    rho = jnp.arange(dests, dtype=jnp.int32) // 2
    members = ((STRIDE * quad + (rho - shift + STRIDE) % STRIDE + shift) % n_z) * 2 + jnp.arange(
        dests, dtype=jnp.int32
    ) % 2
    mine = jnp.stack([me, core]).astype(jnp.int32)

    wide = gate_weight.shape[1]
    chips = n_dp // 2
    rows, pack, downs = pl.pallas_call(
        prep_kernel,
        out_shape=(shape((tok, full)), shape((wide, both)), shape((chips, down_rows, width))),
        in_specs=[whole(pltpu.HBM)] * 6,
        out_specs=(whole(pltpu.HBM),) * 3,
        scratch_shapes=[
            pltpu.VMEM((tok, full), BF16),
            pltpu.VMEM((wide, both), BF16),
            pltpu.VMEM((down_rows, width), BF16),
            pltpu.VMEM((expert_ids.shape[1], tok), jnp.int32),
            pltpu.VMEM((expert_ids.shape[1], tok), BF16),
            pltpu.SemaphoreType.DMA((6,)),
            pltpu.SemaphoreType.DMA((2 + chips,)),
        ],
        compiler_params=params(60),
        name="prep",
    )(grad_out, expert_ids.T, route_weights.T, gate_weight[0], up_weight[0], down_weight[0])
    packs = lax.all_gather(pack, "dp", axis=0, tiled=False)
    same_core = [
        [d * n_expert + e for d in range(c, n_dp, 2)] for c in range(2) for e in range(n_expert)
    ]
    swap = [(d, d ^ 1) for d in range(n_dp)]
    own_down = exchange(downs, axes, same_core)
    blocks = lax.all_gather(rows, axes, axis=0, tiled=True, axis_index_groups=apart)
    send, select = pl.pallas_call(
        functools.partial(select_kernel, cap),
        out_shape=(shape((dests, per, full)), shape((slots, STRIDE * tok))),
        in_specs=[whole(pltpu.SMEM), whole()],
        out_specs=(whole(pltpu.HBM), whole()),
        scratch_shapes=[pltpu.VMEM((dests, per, full), BF16), pltpu.SemaphoreType.DMA((3,))],
        compiler_params=params(16),
        name="select",
    )(members, blocks)
    own_down, send = lax.optimization_barrier((own_down, send))
    other_down = lax.ppermute(own_down, "dp", swap)
    got = exchange(send, axes, near).reshape(slots, full)
    hid, turned, slope, silu = pl.pallas_call(
        functools.partial(act_kernel, cap, down_rows),
        out_shape=(
            shape((slots, hidden)),
            shape((hidden, slots)),
            shape((slots, hidden), F32),
            shape((slots, hidden), F32),
        ),
        in_specs=[whole()],
        out_specs=(whole(),) * 4,
        compiler_params=params(24),
        cost_estimate=pl.CostEstimate(flops=slots * slots * both * 2, bytes_accessed=8 * slots * both, transcendentals=0),
        name="act",
    )(pre)
    back, scaled = pl.pallas_call(
        mid_kernel,
        out_shape=(shape((slots, full)), shape((slots, width))),
        in_specs=[whole(pltpu.SMEM), whole()] + [whole(pltpu.HBM)] * 6,
        out_specs=(whole(pltpu.HBM),) * 2,
        scratch_shapes=[
            pltpu.VMEM((slots, full), BF16),
            pltpu.VMEM((slots, both), BF16),
            pltpu.VMEM((slots, width), BF16),
            pltpu.VMEM((chips, 2, down_rows, width), BF16),
            pltpu.VMEM((slots, hidden), BF16),
            pltpu.VMEM((slots, hidden), F32),
            pltpu.VMEM((slots, hidden), F32),
            pltpu.VMEM((n_dp, wide, both), BF16),
            pltpu.SemaphoreType.DMA((6,)),
            pltpu.SemaphoreType.DMA((5,)),
        ],
        compiler_params=params(50),
        cost_estimate=pl.CostEstimate(flops=6 * slots * hidden * width, bytes_accessed=6 * hidden * width, transcendentals=0),
        name="mid",
    )(mine, got, own_down, other_down, hid, slope, silu, packs)
    scaled, _ = lax.optimization_barrier((scaled, back))
    keep, give = pl.pallas_call(
        down_kernel,
        out_shape=(shape((hidden // 2, width)), shape((hidden // 2, width))),
        in_specs=[whole(pltpu.SMEM), whole(), whole()],
        out_specs=(whole(), whole()),
        compiler_params=params(20),
        cost_estimate=pl.CostEstimate(flops=2 * slots * hidden * width, bytes_accessed=2 * (slots + hidden) * width, transcendentals=0),
        name="down",
    )(mine, scaled, turned)
    taken = lax.ppermute(give, "dp", swap)
    chip_part = (keep.astype(F32) + taken.astype(F32)).astype(BF16)
    down_grad = lax.psum_scatter(
        chip_part,
        "dp",
        scatter_dimension=0,
        tiled=True,
        axis_index_groups=[list(range(c, n_dp, 2)) for c in range(2)],
    )
    back = exchange(back.reshape(dests, per, full), axes, near).reshape(slots, full)
    back, _ = lax.optimization_barrier((back, chip_part))
    place = (me // 2 // STRIDE).reshape(1).astype(jnp.int32)
    cut = (full // META + 1) // 2 * META
    own, after, left, right, before = pl.pallas_call(
        combine_kernel,
        out_shape=(
            shape((tok, full), F32),
            shape((tok, full), F32),
            shape((tok, cut)),
            shape((tok, full - cut)),
            shape((tok, full), F32),
        ),
        in_specs=[whole(pltpu.SMEM), whole(), whole()],
        out_specs=(whole(),) * 5,
        scratch_shapes=[pltpu.VMEM((STRIDE * tok, full), F32)],
        compiler_params=params(12),
        name="combine",
    )(place, select, back)

    def hop(value, step):
        perm = [(e, ((e // 2 + step) % n_z) * 2 + e % 2) for e in range(n_expert)]
        return lax.ppermute(value, "expert", perm)

    parts = [own]
    for name, part, piece, base, step in (("up", after, left, 0, STRIDE), ("down", before, right, cut, -STRIDE)):
        out = pl.pallas_call(
            functools.partial(pass_kernel, base),
            out_shape=shape((tok, full)),
            in_specs=[whole(), whole()],
            out_specs=whole(),
            compiler_params=params(8),
            name="pass_" + name,
        )(part, hop(piece, step))
        parts.append(hop(out, step))
    token_grad, route_grad = pl.pallas_call(
        last_kernel,
        out_shape=(shape((tok, width)), shape(expert_ids.shape[::-1])),
        in_specs=[whole()] * (1 + len(parts)),
        out_specs=(whole(), whole()),
        compiler_params=params(8),
        name="last",
    )(expert_ids.T, *parts)
    return token_grad, route_grad.T, down_grad[None]


def solution(mesh):
    return jax.shard_map(
        functools.partial(per_device, mesh.shape["dp"], mesh.shape["expert"]),
        mesh=mesh,
        in_specs=(
            P(("dp", "expert"), None),
            P(("dp", "expert"), None),
            P(("dp", "expert"), None),
            P("dp", "expert", None, None),
            P("expert", "dp", None),
            P("expert", "dp", None),
            P("expert", "dp", None),
        ),
        out_specs=(P(("dp", "expert"), None), P(("dp", "expert"), None), P("expert", "dp", None)),
        check_vma=False,
    )
```
